32 devices in a mesh: dp: 8 (over z, x), tensor: 4 (over y, core).
Axes of the slice: x: 2, y: 2, z: 4, core: 2. Of those that a mesh axis runs over, the one named last changes fastest.
Arguments:
- inputs: bfloat16 [8192, 6144], P('dp'), may hold values from -6 to 6
- pre_act: bfloat16 [8192, 1024], P('dp', 'tensor'), may hold values from -6 to 6
- grad_hidden: bfloat16 [8192, 1024], P('dp', 'tensor'), may hold values from -6 to 6
- master: float32 [6144, 1024], P('dp', 'tensor'), may hold values from -0.1875 to 0.1875
- moment_one: float32 [6144, 1024], P('dp', 'tensor'), may hold values from -6 to 6
- moment_two: float32 [6144, 1024], P('dp', 'tensor'), may hold values from 1 to 32768
Outputs:
- grad_input: bfloat16 [8192, 6144], P('dp', 'tensor')
- new_master: float32 [6144, 1024], P('dp', 'tensor')
- new_one: float32 [6144, 1024], P('dp', 'tensor')
- new_two: float32 [6144, 1024], P('dp', 'tensor')
- new_weights: bfloat16 [6144, 1024], P(None, 'tensor')
The draws below stay inside these ranges and needn't reach their ends.
All inputs are finite; a program needn't handle non-finite values.
Results may differ from the reference program's by a relative error of at most 0.013.
Values may be sent and summed in bfloat16 or wider, within the bound.
A program may use at most 128 MiB of HBM per device.

```python
import math
import jax
import jax.numpy as jnp
from jax import lax

D = 6144
BUCKET_DEV = 256
TOK_DEV = 1024
QBLOCK = 256
ADAM_STEP = 10
FF_W = 1024
TOKENS = 8192
N_DP = 8
N_TENSOR = 4


def block_scale(own_key, extent, pieces, low, high):
    def one(position, shards_of):
        draws = jax.random.uniform(jax.random.fold_in(jax.random.fold_in(own_key, 6), position), (shards_of,), jnp.float32, low / len(pieces), high / len(pieces))
        return jnp.repeat(jnp.exp(draws), extent[position] // shards_of).reshape((-1,) + (1,) * (len(extent) - position - 1))

    level = one(*pieces[0])
    for cut in pieces[1:]:
        level = level * one(*cut)
    return level


def scatter_about(own_key, extent, width, reach, cuts=(), kind=jnp.bfloat16):
    factor_of = block_scale(own_key, extent, cuts, -0.22, 0.18) if cuts else 1.0
    entries = jax.random.normal(own_key, extent, jnp.float32) * width * factor_of
    return jnp.minimum(jnp.maximum(entries, -reach), reach).astype(kind)


def setup_inputs(seed: int = 0) -> dict:
    splits = jax.random.split(jax.random.key(seed), 7)
    return {
        "inputs": scatter_about(splits[0], (TOKENS, D), 1.0, 6.0, ((0, 8),)),
        "pre_act": scatter_about(splits[1], (TOKENS, FF_W), 1.0, 6.0, ((0, 8), (1, 4))),
        "grad_hidden": scatter_about(splits[2], (TOKENS, FF_W), 1.0, 6.0, ((0, 8), (1, 4))),
        "master": scatter_about(splits[3], (D, FF_W), FF_W ** -0.5, 0.1875, ((0, 8), (1, 4)), jnp.float32),
        "moment_one": scatter_about(splits[4], (D, FF_W), 1.0, 6.0, ((0, 8), (1, 4)), jnp.float32),
        "moment_two": jnp.clip(jnp.exp(math.log(32768.0) - 10.3972077 * jax.random.uniform(splits[5], (D, FF_W), jnp.float32) ** block_scale(splits[5], (D, FF_W), ((0, 8), (1, 4)), -0.2, 0.2)), 1.0, 32768.0),
    }


def gelu_slope(value):
    cdf = 0.5 * (1.0 + jax.scipy.special.erf(value / math.sqrt(2.0)))
    pdf = jnp.exp(-0.5 * value * value) / math.sqrt(2.0 * math.pi)
    return cdf + value * pdf

def quant_round(term):
    rows, cols = term.shape
    blocks = term.reshape(rows, cols // QBLOCK, QBLOCK)
    scale = (lax.optimization_barrier(jnp.max(jnp.abs(blocks), axis=2)) + 1e-06) / 127.0
    codes = jnp.clip(blocks / scale[:, :, None], -127.0, 127.0).astype(jnp.bfloat16)
    return (codes.astype(jnp.float32) * scale[:, :, None]).reshape(rows, cols)

def reference(inputs, pre_act, grad_hidden, master, moment_one, moment_two):
    act_grad = (grad_hidden.astype(jnp.float32) * gelu_slope(pre_act.astype(jnp.float32))).astype(jnp.bfloat16)
    weights = master.astype(jnp.bfloat16)
    act_blocks = act_grad.reshape(N_DP, TOK_DEV, FF_W)
    in_blocks = inputs.reshape(N_DP, TOK_DEV, D)

    def input_block(act_rows):
        total = jnp.zeros((TOK_DEV, D), jnp.float32)
        for index in range(N_TENSOR):
            cols = act_rows[:, index * BUCKET_DEV:(index + 1) * BUCKET_DEV]
            wcols = weights[:, index * BUCKET_DEV:(index + 1) * BUCKET_DEV]
            part = jnp.dot(cols, wcols.T, preferred_element_type=jnp.float32)
            total = total + part.astype(jnp.bfloat16).astype(jnp.float32)
        return total.astype(jnp.bfloat16)
    grad_input = lax.map(input_block, act_blocks).reshape(TOKENS, D)

    def add_term(carry, pair):
        term = jnp.dot(pair[0].T, pair[1], preferred_element_type=jnp.float32)
        return (carry + quant_round(term), None)
    grad, unused = lax.scan(add_term, jnp.zeros((D, FF_W), jnp.float32), (in_blocks, act_blocks))
    new_one = 0.9 * moment_one + 0.1 * grad
    new_two = 0.999 * moment_two + 0.001 * grad * grad
    corr_one = 1.0 - 0.9 ** ADAM_STEP
    corr_two = 1.0 - 0.999 ** ADAM_STEP
    update = new_one / corr_one / (jnp.sqrt(new_two / corr_two) + 1e-08) + 0.01 * master
    new_master = master - 0.01 * update
    return (grad_input, new_master, new_one, new_two, new_master.astype(jnp.bfloat16))
```

```python
import functools
import math

import jax
import jax.numpy as jnp
from jax import lax
from jax.experimental import pallas as pl
from jax.experimental.pallas import tpu as pltpu
from jax.sharding import PartitionSpec as P

QBLOCK = 256
ADAM_STEP = 10
Z, X, T = 4, 2, 4
W_SPLIT = 464
G_SPLIT = 160
N_SPLIT = 640
MESH = pl.DeviceIdType.MESH
F32, BF16 = jnp.float32, jnp.bfloat16


def gelu_slope(value):
    cdf = 0.5 * (1.0 + lax.erf(value * (1.0 / math.sqrt(2.0))))
    pdf = jnp.exp(-0.5 * value * value) / math.sqrt(2.0 * math.pi)
    return cdf + value * pdf


def encode(term):
    rows, cols = term.shape
    blocks = term.reshape(rows, cols // QBLOCK, QBLOCK)
    scale = (jnp.max(jnp.abs(blocks), axis=2) + 1e-06) / 127.0
    codes = jnp.clip(blocks / scale[:, :, None], -127.0, 127.0).astype(BF16)
    return (codes.reshape(rows, cols), scale)


def decode(codes, scale):
    rows, cols = codes.shape
    blocks = codes.astype(F32).reshape(rows, cols // QBLOCK, QBLOCK)
    return (blocks * scale[:, :, None]).reshape(rows, cols)


def adam(grad, master, moment_one, moment_two):
    new_one = 0.9 * moment_one + 0.1 * grad
    new_two = 0.999 * moment_two + 0.001 * grad * grad
    corr_one = 1.0 - 0.9**ADAM_STEP
    corr_two = 1.0 - 0.999**ADAM_STEP
    update = new_one / corr_one / (jnp.sqrt(new_two / corr_two) + 1e-08) + 0.01 * master
    return master - 0.01 * update, new_one, new_two


def kernel(
    in_hbm, pre_ref, hid_ref, master_ref, one_ref, two_ref,
    gi_ref, nm_ref, n1_ref, n2_ref, nw_ref,
    xin, w_buf, wx, act, act_t, term, xr, zua, zda, sua, sda, zub, zdb, sub, sdb, fxs, fxr, grad_t,
    in_sem, act_s, act_r, ws, wr, wag, nag, rxs, rxr, ras, rar, rbs, rbr, fs, fr,
):
    r = lax.axis_index("dp")
    k = lax.axis_index("tensor")
    z, x = r // X, r % X
    o = 1 - x
    across, above, below = {"dp": r + 1 - 2 * x}, {"dp": r + X}, {"dp": r - X}
    up_ok, dn_ok = z <= Z - 2, z >= 1
    tok, hid = pre_ref.shape
    rows = master_ref.shape[0]
    pend = []

    def when(cond, fn):
        if cond is None:
            fn()
        else:
            pl.when(cond)(fn)

    def rc(src, dst, ssem, rsem, dev):
        return pltpu.make_async_remote_copy(
            src_ref=src, dst_ref=dst, send_sem=ssem, recv_sem=rsem, device_id=dev, device_id_type=MESH
        )

    def send(cond, make):
        when(cond, lambda: make().start())
        pend.append((cond, make))

    def got(cond, make):
        when(cond, lambda: make().wait_recv())

    class Gather:
        def __init__(self, buf, sems, split, on_block):
            self.buf, self.s, self.split, self.on = buf, sems, split, on_block

        def a(self, zz, xx):
            return self.buf.at[X * zz + xx, pl.ds(0, self.split), :]

        def b(self, zz):
            return self.buf.at[pl.ds(X * zz, X), pl.ds(self.split, rows - self.split), :]

        def b1(self, zz, xx):
            return self.buf.at[X * zz + xx, pl.ds(self.split, rows - self.split), :]

        def mk(self, ref, idx, dev):
            return lambda: rc(ref(), ref(), self.s.at[0, idx], self.s.at[1, idx], dev)

        def za(self, s):
            zz_u, zz_d = z - s, z + s
            send(up_ok & (zz_u >= 0), self.mk(lambda: self.a(zz_u, x), s, above))
            send(dn_ok & (zz_d <= Z - 1), self.mk(lambda: self.a(zz_d, x), 3 + s, below))

        def zb(self, s):
            zz_u, zz_d = z - s, z + s
            send(up_ok & (zz_u >= 0), self.mk(lambda: self.b(zz_u), 6 + s, above))
            send(dn_ok & (zz_d <= Z - 1), self.mk(lambda: self.b(zz_d), 9 + s, below))

        def xa(self, cond, zz):
            send(cond, self.mk(lambda: self.a(zz, x), 12 + zz, across))

        def start(self):
            self.xa(None, z)
            self.za(0)
            send(None, self.mk(lambda: self.b1(z, x), 16, across))
            self.on(None, z, x, 0)

        def part_a(self, s):
            zu, zd = z - 1 - s, z + 1 + s
            cu, cd = zu >= 0, zd <= Z - 1
            got(cu, self.mk(lambda: self.a(zu, x), s, above))
            got(cd, self.mk(lambda: self.a(zd, x), 3 + s, below))
            if s + 1 < Z - 1:
                self.za(s + 1)
            self.xa(cu, zu)
            self.xa(cd, zd)
            self.on(cu, zu, x, 0)
            self.on(cd, zd, x, 0)

        def part_b(self, s):
            if s == 0:
                got(None, self.mk(lambda: self.b1(z, o), 16, across))
            else:
                zu, zd = z - s, z + s
                cu, cd = zu >= 0, zd <= Z - 1
                got(cu, self.mk(lambda: self.b(zu), 6 + s - 1, above))
                got(cd, self.mk(lambda: self.b(zd), 9 + s - 1, below))
            if s < Z - 1:
                self.zb(s)
            if s == 0:
                for xx in range(X):
                    self.on(None, z, xx, 1)
            else:
                for xx in range(X):
                    self.on(cu, zu, xx, 1)
                    self.on(cd, zd, xx, 1)

        def finish_x(self):
            for j in range(Z):
                zz = (z + j) % Z
                got(None, self.mk(lambda: self.a(zz, o), 12 + zz, across))
                self.on(None, zz, o, 0)

    def w_part(ref, idx, xx, part):
        lo, n = (0, W_SPLIT) if part == 0 else (W_SPLIT, rows - W_SPLIT)
        return ref.at[idx, xx, pl.ds(lo, n), :]

    def to_tensor(cond, zz, xx, part):
        lo, n = (0, W_SPLIT) if part == 0 else (W_SPLIT, rows - W_SPLIT)
        sem = (zz * X + xx) * 2 + part
        rsem = (k * X + xx) * 2 + part
        c = zz != k
        send(
            c if cond is None else cond & c,
            lambda: rc(
                w_buf.at[X * zz + xx, pl.ds(lo, n), :], w_part(wx, k, xx, part),
                ws.at[sem], wr.at[rsem], {"tensor": zz},
            ),
        )

    gw = Gather(w_buf, wag, W_SPLIT, to_tensor)
    gn = Gather(nw_ref, nag, N_SPLIT, lambda *_: None)

    hi = z // 2
    order = [3 - 3 * hi, 2 - hi, 1 - z + 4 * hi, z]

    def fetch(j):
        blk = X * order[j // 2] + (o if j % 2 == 0 else x)
        col = pl.multiple_of(blk * rows, 128)
        return pltpu.make_async_copy(in_hbm.at[:, pl.ds(col, rows)], xin.at[j], in_sem.at[j])

    for j in range(Z * X):
        fetch(j).start()
    w_buf[r] = master_ref[...].astype(BF16)

    barrier = pltpu.get_barrier_semaphore()

    def hello(dev):
        pl.semaphore_signal(barrier, inc=1, device_id=dev, device_id_type=MESH)

    hello(across)
    when(up_ok, lambda: hello(above))
    when(dn_ok, lambda: hello(below))
    for j in range(1, T):
        hello({"tensor": (k + j) % T})
    pl.semaphore_wait(barrier, T + 1 + z * (Z - 1 - z) // 2)

    gw.start()

    step_t = 256

    @pl.loop(0, tok // step_t)
    def _(i):
        here = pl.ds(pl.multiple_of(i * step_t, step_t), step_t)
        val = hid_ref[here, :].astype(F32) * gelu_slope(pre_ref[here, :].astype(F32))
        act[k, here, :] = val.astype(BF16)
        act_t[:, here] = val.T.astype(BF16)

    def make_term(j):
        blk = X * order[j // 2] + (o if j % 2 == 0 else x)
        fetch(j).wait()

        @pl.loop(0, rows // 256)
        def _(c):
            cols = pl.ds(pl.multiple_of(c * 256, 256), 256)
            t = jnp.dot(act_t[...], xin[j, :, cols], preferred_element_type=F32)
            scale = (jnp.max(jnp.abs(t), axis=0, keepdims=True) + 1e-06) / 127.0
            codes = jnp.clip(t / scale, -127.0, 127.0).astype(BF16)
            term[blk, :, cols] = (codes.astype(F32) * scale).astype(BF16)

    def xr_copy(t, own):
        return lambda: rc(
            term.at[X * t + own, pl.ds(0, G_SPLIT), :], xr.at[t], rxs.at[t], rxr.at[t], across
        )

    for i in range(Z):
        make_term(2 * i)
        send(None, xr_copy(order[i], o))
        make_term(2 * i + 1)
        if i == 0:
            for j in range(1, T):
                kk = (k + j) % T
                send(
                    None,
                    lambda kk=kk, j=j: rc(
                        act.at[k], act.at[k], act_s.at[j - 1], act_r.at[j - 1], {"tensor": kk}
                    ),
                )

    def z_sum(s, value, arrived, zu, zd, su, sd, ssem, rsem):
        tu, td = z + 3 - s, z - 3 + s
        cu, cd = up_ok & (z <= s), dn_ok & (z >= 3 - s)
        for cond, edge, t, zin, out, base, dev in (
            (cu, z == 0, tu, zu, su, 0, above),
            (cd, z == Z - 1, td, zd, sd, 3, below),
        ):
            make = lambda zin=zin, out=out, base=base, dev=dev: rc(
                out.at[s], zin.at[s], ssem.at[base + s], rsem.at[base + s], dev
            )
            def body(edge=edge, t=t, zin=zin, out=out, base=base, dev=dev, make=make):
                arrived(t)
                own = value(t)

                @pl.when(edge)
                def _():
                    out[s] = own().astype(BF16)

                if s > 0:
                    @pl.when(jnp.logical_not(edge))
                    def _():
                        rc(out.at[s], zin.at[s - 1], ssem.at[base + s - 1], rsem.at[base + s - 1], dev).wait_recv()
                        out[s] = (own() + zin[s - 1].astype(F32)).astype(BF16)

            pl.when(cond)(body)
            send(cond, make)

    def value_a(t):
        return lambda: term[X * t + x, :G_SPLIT, :].astype(F32) + xr[t].astype(F32)

    def value_b(t):
        return lambda: term[pl.ds(X * t, X), G_SPLIT:, :].astype(F32)

    def arrived_a(t):
        xr_copy(t, o)().wait_recv()

    def sum_a(s):
        z_sum(s, value_a, arrived_a, zua, zda, sua, sda, ras, rar)

    def sum_b(s):
        z_sum(s, value_b, lambda t: None, zub, zdb, sub, sdb, rbs, rbr)

    sum_b(0)
    gw.part_b(0)
    for s in range(Z - 1):
        sum_a(s)
        gw.part_a(s)
        if s + 1 < Z - 1:
            sum_b(s + 1)
        gw.part_b(s + 1)

    last = Z - 2
    sb = fxs
    sb[...] = term[pl.ds(X * z, X), G_SPLIT:, :].astype(F32)
    for cond, zin, base, dev in ((dn_ok, zub, 0, above), (up_ok, zdb, 3, below)):
        def body(zin=zin, base=base, dev=dev):
            rc(zin.at[last], zin.at[last], rbs.at[base + last], rbr.at[base + last], dev).wait_recv()
            sb[...] += zin[last].astype(F32)
        pl.when(cond)(body)
    fxr[0] = sb[o].astype(BF16)
    fx = lambda: rc(fxr.at[0], fxr.at[1], fs, fr, across)
    send(None, fx)
    arrived_a(z)
    grad_t[:G_SPLIT, :] = value_a(z)()
    for cond, zin, base, dev in ((dn_ok, zua, 0, above), (up_ok, zda, 3, below)):
        def body(zin=zin, base=base, dev=dev):
            rc(zin.at[last], zin.at[last], ras.at[base + last], rar.at[base + last], dev).wait_recv()
            grad_t[:G_SPLIT, :] += zin[last].astype(F32)
        pl.when(cond)(body)
    fx().wait_recv()
    grad_t[G_SPLIT:, :] = sb[x] + fxr[1].astype(F32)

    @pl.loop(0, rows // 256)
    def _(c):
        here = pl.ds(pl.multiple_of(c * 256, 256), 256)
        nm, n1, n2 = adam(
            grad_t[:, here].T, master_ref[here, :], one_ref[here, :], two_ref[here, :]
        )
        nm_ref[here, :] = nm
        n1_ref[here, :] = n1
        n2_ref[here, :] = n2
        nw_ref[r, here, :] = nm.astype(BF16)

    gn.start()
    gw.finish_x()
    for s in range(Z - 1):
        gn.part_b(s)
        gn.part_a(s)
    gn.part_b(Z - 1)

    wx[k] = w_buf[pl.ds(X * k, X)]
    for j in range(1, T):
        src = (k + T - j) % T
        got(None, lambda: rc(act.at[src], act.at[src], act_s.at[j - 1], act_r.at[j - 1], {"tensor": src}))
        for xx in range(X):
            for part in range(2):
                got(
                    None,
                    lambda: rc(
                        w_part(wx, src, xx, part), w_part(wx, src, xx, part),
                        ws.at[0], wr.at[(src * X + xx) * 2 + part], {"tensor": src},
                    ),
                )

    @pl.loop(0, tok // step_t)
    def _(i):
        here = pl.ds(pl.multiple_of(i * step_t, step_t), step_t)
        for xx in range(X):
            total = None
            for src in range(T):
                part = lax.dot_general(
                    act[src, here, :], wx[src, xx], (((1,), (1,)), ((), ())), preferred_element_type=F32
                )
                total = part if total is None else total + part
            gi_ref[here, xx * rows:(xx + 1) * rows] = total.astype(BF16)

    gn.finish_x()
    for cond, make in pend:
        when(cond, lambda: make().wait_send())


def local_kernel(inputs, pre_act, grad_hidden, master, moment_one, moment_two):
    tok, hid = pre_act.shape
    rows = master.shape[0]
    n = Z * X
    gb = hid - G_SPLIT
    vmem = pl.BlockSpec(memory_space=pltpu.VMEM)
    dma = pltpu.SemaphoreType.DMA
    out = pl.pallas_call(
        kernel,
        out_shape=(
            jax.ShapeDtypeStruct((tok, rows * X), BF16),
            jax.ShapeDtypeStruct((rows, hid), F32),
            jax.ShapeDtypeStruct((rows, hid), F32),
            jax.ShapeDtypeStruct((rows, hid), F32),
            jax.ShapeDtypeStruct((n, rows, hid), BF16),
        ),
        in_specs=[pl.BlockSpec(memory_space=pl.ANY)] + [vmem] * 5,
        out_specs=[vmem] * 5,
        scratch_shapes=[
            pltpu.VMEM((n, tok, rows), BF16),
            pltpu.VMEM((n, rows, hid), BF16),
            pltpu.VMEM((T, X, rows, hid), BF16),
            pltpu.VMEM((T, tok, hid), BF16),
            pltpu.VMEM((hid, tok), BF16),
            pltpu.VMEM((n, hid, rows), BF16),
            pltpu.VMEM((Z, G_SPLIT, rows), BF16),
            *[pltpu.VMEM((Z - 1, G_SPLIT, rows), BF16)] * 4,
            *[pltpu.VMEM((Z - 1, X, gb, rows), BF16)] * 4,
            pltpu.VMEM((X, gb, rows), F32),
            pltpu.VMEM((2, gb, rows), BF16),
            pltpu.VMEM((hid, rows), F32),
            dma((n,)), dma((T - 1,)), dma((T - 1,)),
            dma((Z * X * 2,)), dma((T * X * 2,)),
            dma((2, 17)), dma((2, 17)),
            dma((Z,)), dma((Z,)),
            dma((6,)), dma((6,)), dma((6,)), dma((6,)),
            dma(()), dma(()),
        ],
        compiler_params=pltpu.CompilerParams(
            collective_id=0, has_side_effects=True, vmem_limit_bytes=60 * 1024 * 1024
        ),
        cost_estimate=pl.CostEstimate(
            flops=4 * tok * rows * n * hid, bytes_accessed=2 * tok * rows * n * 2, transcendentals=tok * hid
        ),
    )(inputs, pre_act, grad_hidden, master, moment_one, moment_two)
    return (*out[:4], out[4].reshape(n * rows, hid))


def local_plain(inputs, pre_act, grad_hidden, master, moment_one, moment_two):
    act_grad = (grad_hidden.astype(F32) * gelu_slope(pre_act.astype(F32))).astype(BF16)
    weights = lax.all_gather(master.astype(BF16), "dp", axis=0, tiled=True)
    rows = lax.all_to_all(weights, "tensor", split_axis=0, concat_axis=1, tiled=True)
    acts = lax.all_gather(act_grad, "tensor", axis=1, tiled=True)
    grad_input = jnp.einsum("th,dh->td", acts, rows, preferred_element_type=F32).astype(BF16)
    term = jnp.einsum("tr,th->rh", inputs, act_grad, preferred_element_type=F32)
    codes, scale = encode(term)
    grad = lax.psum_scatter(decode(codes, scale), "dp", scatter_dimension=0, tiled=True)
    new_master, new_one, new_two = adam(grad, master, moment_one, moment_two)
    new_weights = lax.all_gather(new_master.astype(BF16), "dp", axis=0, tiled=True)
    return (grad_input, new_master, new_one, new_two, new_weights)


def solution(mesh):
    sizes = dict(mesh.shape)
    body = local_kernel if sizes == {"dp": Z * X, "tensor": T} else local_plain
    two = P("dp", "tensor")
    return jax.shard_map(
        body,
        mesh=mesh,
        in_specs=(P("dp", None), two, two, two, two, two),
        out_specs=(two, two, two, two, P(None, "tensor")),
        check_vma=False,
    )
```

```python
import functools
import math

import jax
import jax.numpy as jnp
from jax import lax
from jax.experimental import pallas as pl
from jax.experimental.pallas import tpu as pltpu
from jax.sharding import PartitionSpec as P

QBLOCK = 256
ADAM_STEP = 10
Z, X, T = 4, 2, 4
W_SPLIT = 544
G_SPLIT = 160
N_SPLIT = 576
MESH = pl.DeviceIdType.MESH
F32, BF16 = jnp.float32, jnp.bfloat16


def gelu_slope(value):
    cdf = 0.5 * (1.0 + lax.erf(value * (1.0 / math.sqrt(2.0))))
    pdf = jnp.exp(-0.5 * value * value) / math.sqrt(2.0 * math.pi)
    return cdf + value * pdf


def encode(term):
    rows, cols = term.shape
    blocks = term.reshape(rows, cols // QBLOCK, QBLOCK)
    scale = (jnp.max(jnp.abs(blocks), axis=2) + 1e-06) / 127.0
    codes = jnp.clip(blocks / scale[:, :, None], -127.0, 127.0).astype(BF16)
    return (codes.reshape(rows, cols), scale)


def decode(codes, scale):
    rows, cols = codes.shape
    blocks = codes.astype(F32).reshape(rows, cols // QBLOCK, QBLOCK)
    return (blocks * scale[:, :, None]).reshape(rows, cols)


def adam(grad, master, moment_one, moment_two):
    new_one = 0.9 * moment_one + 0.1 * grad
    new_two = 0.999 * moment_two + 0.001 * grad * grad
    corr_one = 1.0 - 0.9**ADAM_STEP
    corr_two = 1.0 - 0.999**ADAM_STEP
    update = new_one / corr_one / (jnp.sqrt(new_two / corr_two) + 1e-08) + 0.01 * master
    return master - 0.01 * update, new_one, new_two


def kernel(
    in_hbm, pre_ref, hid_ref, master_ref, one_hbm, two_hbm,
    gi_hbm, grad_hbm, nw_hbm,
    gi_ref, grad_ref, nw_ref, one_ref, two_ref,
    xin, w_buf, wx, act, act_t, term, xr, zua, zda, sua, sda, zub, zdb, sub, sdb, fxs, fxr, grad_t,
    out_sem, mom_sem, in_sem, act_s, act_r, ws, wr, wag, nag, rxs, rxr, ras, rar, rbs, rbr, fs, fr,
):
    r = lax.axis_index("dp")
    k = lax.axis_index("tensor")
    z, x = r // X, r % X
    o = 1 - x
    across, above, below = {"dp": r + 1 - 2 * x}, {"dp": r + X}, {"dp": r - X}
    up_ok, dn_ok = z <= Z - 2, z >= 1
    tok, hid = pre_ref.shape
    rows = master_ref.shape[0]
    pend = []

    def when(cond, fn):
        if cond is None:
            fn()
        else:
            pl.when(cond)(fn)

    def rc(src, dst, ssem, rsem, dev):
        return pltpu.make_async_remote_copy(
            src_ref=src, dst_ref=dst, send_sem=ssem, recv_sem=rsem, device_id=dev, device_id_type=MESH
        )

    def send(cond, make):
        when(cond, lambda: make().start())
        pend.append((cond, make))

    def got(cond, make):
        when(cond, lambda: make().wait_recv())

    class Gather:
        def __init__(self, buf, sems, split, on_block):
            self.buf, self.s, self.split, self.on = buf, sems, split, on_block

        def a(self, zz, xx):
            return self.buf.at[X * zz + xx, pl.ds(0, self.split), :]

        def b(self, zz):
            return self.buf.at[pl.ds(X * zz, X), pl.ds(self.split, rows - self.split), :]

        def b1(self, zz, xx):
            return self.buf.at[X * zz + xx, pl.ds(self.split, rows - self.split), :]

        def mk(self, ref, idx, dev):
            return lambda: rc(ref(), ref(), self.s.at[0, idx], self.s.at[1, idx], dev)

        def za(self, s):
            zz_u, zz_d = z - s, z + s
            send(up_ok & (zz_u >= 0), self.mk(lambda: self.a(zz_u, x), s, above))
            send(dn_ok & (zz_d <= Z - 1), self.mk(lambda: self.a(zz_d, x), 3 + s, below))

        def zb(self, s):
            zz_u, zz_d = z - s, z + s
            send(up_ok & (zz_u >= 0), self.mk(lambda: self.b(zz_u), 6 + s, above))
            send(dn_ok & (zz_d <= Z - 1), self.mk(lambda: self.b(zz_d), 9 + s, below))

        def xa(self, cond, zz):
            send(cond, self.mk(lambda: self.a(zz, x), 12 + zz, across))

        def start(self):
            self.xa(None, z)
            self.za(0)
            send(None, self.mk(lambda: self.b1(z, x), 16, across))
            self.on(None, z, x, 0)

        def part_a(self, s):
            zu, zd = z - 1 - s, z + 1 + s
            cu, cd = zu >= 0, zd <= Z - 1
            got(cu, self.mk(lambda: self.a(zu, x), s, above))
            got(cd, self.mk(lambda: self.a(zd, x), 3 + s, below))
            if s + 1 < Z - 1:
                self.za(s + 1)
            self.xa(cu, zu)
            self.xa(cd, zd)
            self.on(cu, zu, x, 0)
            self.on(cd, zd, x, 0)

        def part_b(self, s):
            if s == 0:
                got(None, self.mk(lambda: self.b1(z, o), 16, across))
            else:
                zu, zd = z - s, z + s
                cu, cd = zu >= 0, zd <= Z - 1
                got(cu, self.mk(lambda: self.b(zu), 6 + s - 1, above))
                got(cd, self.mk(lambda: self.b(zd), 9 + s - 1, below))
            if s < Z - 1:
                self.zb(s)
            if s == 0:
                for xx in range(X):
                    self.on(None, z, xx, 1)
            else:
                for xx in range(X):
                    self.on(cu, zu, xx, 1)
                    self.on(cd, zd, xx, 1)

        def finish_x(self, *only):
            for j in only or range(Z):
                zz = (z + j) % Z
                got(None, self.mk(lambda: self.a(zz, o), 12 + zz, across))
                self.on(None, zz, o, 0)

    def w_part(ref, idx, xx, part):
        lo, n = (0, W_SPLIT) if part == 0 else (W_SPLIT, rows - W_SPLIT)
        return ref.at[idx, xx, pl.ds(lo, n), :]

    def to_tensor(cond, zz, xx, part):
        lo, n = (0, W_SPLIT) if part == 0 else (W_SPLIT, rows - W_SPLIT)
        sem = (zz * X + xx) * 2 + part
        rsem = (k * X + xx) * 2 + part
        c = zz != k
        send(
            c if cond is None else cond & c,
            lambda: rc(
                w_buf.at[X * zz + xx, pl.ds(lo, n), :], w_part(wx, k, xx, part),
                ws.at[sem], wr.at[rsem], {"tensor": zz},
            ),
        )

    gw = Gather(w_buf, wag, W_SPLIT, to_tensor)
    gn = Gather(nw_ref, nag, N_SPLIT, lambda *_: None)

    hi = z // 2
    order = [3 - 3 * hi, 2 - hi, 1 - z + 4 * hi, z]

    def fetch(j):
        blk = X * order[j // 2] + (o if j % 2 == 0 else x)
        col = pl.multiple_of(blk * rows, 128)
        return pltpu.make_async_copy(in_hbm.at[:, pl.ds(col, rows)], xin.at[j], in_sem.at[j])

    for j in range(Z * X):
        fetch(j).start()
    moments = [
        pltpu.make_async_copy(one_hbm, one_ref, mom_sem.at[0]),
        pltpu.make_async_copy(two_hbm, two_ref, mom_sem.at[1]),
    ]
    for c in moments:
        c.start()
    w_buf[r] = master_ref[...].astype(BF16)

    barrier = pltpu.get_barrier_semaphore()

    def hello(dev):
        pl.semaphore_signal(barrier, inc=1, device_id=dev, device_id_type=MESH)

    hello(across)
    when(up_ok, lambda: hello(above))
    when(dn_ok, lambda: hello(below))
    for j in range(1, T):
        hello({"tensor": (k + j) % T})
    pl.semaphore_wait(barrier, T + 1 + z * (Z - 1 - z) // 2)

    gw.start()

    step_t = 256

    @pl.loop(0, tok // step_t)
    def _(i):
        here = pl.ds(pl.multiple_of(i * step_t, step_t), step_t)
        val = hid_ref[here, :].astype(F32) * gelu_slope(pre_ref[here, :].astype(F32))
        act[k, here, :] = val.astype(BF16)
        act_t[:, here] = val.T.astype(BF16)

    def make_term(j):
        blk = X * order[j // 2] + (o if j % 2 == 0 else x)
        fetch(j).wait()

        @pl.loop(0, rows // 256)
        def _(c):
            cols = pl.ds(pl.multiple_of(c * 256, 256), 256)
            t = jnp.dot(act_t[...], xin[j, :, cols], preferred_element_type=F32)
            scale = (jnp.max(jnp.abs(t), axis=0, keepdims=True) + 1e-06) / 127.0
            codes = jnp.clip(t / scale, -127.0, 127.0).astype(BF16)
            term[blk, :, cols] = (codes.astype(F32) * scale).astype(BF16)

    def xr_copy(t, own):
        return lambda: rc(
            term.at[X * t + own, pl.ds(0, G_SPLIT), :], xr.at[t], rxs.at[t], rxr.at[t], across
        )

    for i in range(Z):
        make_term(2 * i)
        send(None, xr_copy(order[i], o))
        make_term(2 * i + 1)
        if i == 0:
            for j in range(1, T):
                kk = (k + j) % T
                send(
                    None,
                    lambda kk=kk, j=j: rc(
                        act.at[k], act.at[k], act_s.at[j - 1], act_r.at[j - 1], {"tensor": kk}
                    ),
                )

    def z_sum(s, value, arrived, zu, zd, su, sd, ssem, rsem):
        tu, td = z + 3 - s, z - 3 + s
        cu, cd = up_ok & (z <= s), dn_ok & (z >= 3 - s)
        for cond, edge, t, zin, out, base, dev in (
            (cu, z == 0, tu, zu, su, 0, above),
            (cd, z == Z - 1, td, zd, sd, 3, below),
        ):
            make = lambda zin=zin, out=out, base=base, dev=dev: rc(
                out.at[s], zin.at[s], ssem.at[base + s], rsem.at[base + s], dev
            )
            def body(edge=edge, t=t, zin=zin, out=out, base=base, dev=dev, make=make):
                arrived(t)
                own = value(t)

                @pl.when(edge)
                def _():
                    out[s] = own().astype(BF16)

                if s > 0:
                    @pl.when(jnp.logical_not(edge))
                    def _():
                        rc(out.at[s], zin.at[s - 1], ssem.at[base + s - 1], rsem.at[base + s - 1], dev).wait_recv()
                        out[s] = (own() + zin[s - 1].astype(F32)).astype(BF16)

            pl.when(cond)(body)
            send(cond, make)

    def value_a(t):
        return lambda: term[X * t + x, :G_SPLIT, :].astype(F32) + xr[t].astype(F32)

    def value_b(t):
        return lambda: term[pl.ds(X * t, X), G_SPLIT:, :].astype(F32)

    def arrived_a(t):
        xr_copy(t, o)().wait_recv()

    def sum_a(s):
        z_sum(s, value_a, arrived_a, zua, zda, sua, sda, ras, rar)

    def sum_b(s):
        z_sum(s, value_b, lambda t: None, zub, zdb, sub, sdb, rbs, rbr)

    sum_b(0)
    gw.part_b(0)
    sum_a(0)
    gw.part_a(0)
    sum_b(1)
    sum_a(1)
    sum_b(2)
    sum_a(2)
    gw.part_b(1)

    last = Z - 2
    sb = fxs
    sb[...] = term[pl.ds(X * z, X), G_SPLIT:, :].astype(F32)
    for cond, zin, base, dev in ((dn_ok, zub, 0, above), (up_ok, zdb, 3, below)):
        def body(zin=zin, base=base, dev=dev):
            rc(zin.at[last], zin.at[last], rbs.at[base + last], rbr.at[base + last], dev).wait_recv()
            sb[...] += zin[last].astype(F32)
        pl.when(cond)(body)
    fxr[0] = sb[o].astype(BF16)
    fx = lambda: rc(fxr.at[0], fxr.at[1], fs, fr, across)
    send(None, fx)
    gw.part_a(1)
    arrived_a(z)
    grad_t[:G_SPLIT, :] = value_a(z)()
    for cond, zin, base, dev in ((dn_ok, zua, 0, above), (up_ok, zda, 3, below)):
        def body(zin=zin, base=base, dev=dev):
            rc(zin.at[last], zin.at[last], ras.at[base + last], rar.at[base + last], dev).wait_recv()
            grad_t[:G_SPLIT, :] += zin[last].astype(F32)
        pl.when(cond)(body)
    fx().wait_recv()
    grad_t[G_SPLIT:, :] = sb[x] + fxr[1].astype(F32)

    for c in moments:
        c.wait()

    @pl.loop(0, rows // 256)
    def _(c):
        here = pl.ds(pl.multiple_of(c * 256, 256), 256)
        grad = grad_t[:, here].T
        grad_ref[here, :] = grad
        new_master = adam(grad, master_ref[here, :], one_ref[here, :], two_ref[here, :])[0]
        nw_ref[r, here, :] = new_master.astype(BF16)

    gn.start()
    grad_out = pltpu.make_async_copy(grad_ref, grad_hbm, mom_sem.at[0])
    grad_out.start()
    gw.part_b(2)
    gw.part_a(2)
    gn.part_b(0)
    gn.part_a(0)
    gw.part_b(3)
    gn.part_b(1)
    gn.part_a(1)
    gw.finish_x()
    gn.part_b(2)
    gn.part_a(2)
    gn.part_b(3)

    wx[k] = w_buf[pl.ds(X * k, X)]
    for j in range(1, T):
        src = (k + T - j) % T
        got(None, lambda: rc(act.at[src], act.at[src], act_s.at[j - 1], act_r.at[j - 1], {"tensor": src}))
        for xx in range(X):
            for part in range(2):
                got(
                    None,
                    lambda: rc(
                        w_part(wx, src, xx, part), w_part(wx, src, xx, part),
                        ws.at[0], wr.at[(src * X + xx) * 2 + part], {"tensor": src},
                    ),
                )

    writes = []

    def write(src, dst):
        c = pltpu.make_async_copy(src, dst, out_sem.at[len(writes)])
        c.start()
        writes.append(c)

    for i in range(tok // step_t):
        here = pl.ds(i * step_t, step_t)
        for xx in range(X):
            total = None
            for src in range(T):
                part = lax.dot_general(
                    act[src, here, :], wx[src, xx], (((1,), (1,)), ((), ())), preferred_element_type=F32
                )
                total = part if total is None else total + part
            gi_ref[here, xx * rows:(xx + 1) * rows] = total.astype(BF16)
        write(gi_ref.at[here, :], gi_hbm.at[here, :])

    for j in range(Z):
        gn.finish_x(j)
        both = pl.ds(X * ((z + j) % Z), X)
        write(nw_ref.at[both], nw_hbm.at[both])
    for c in writes:
        c.wait()
    grad_out.wait()
    for cond, make in pend:
        when(cond, lambda: make().wait_send())


def local_kernel(inputs, pre_act, grad_hidden, master, moment_one, moment_two):
    tok, hid = pre_act.shape
    rows = master.shape[0]
    n = Z * X
    gb = hid - G_SPLIT
    vmem = pl.BlockSpec(memory_space=pltpu.VMEM)
    dma = pltpu.SemaphoreType.DMA
    anywhere = pl.BlockSpec(memory_space=pl.ANY)
    grad_input, grad, new_weights = pl.pallas_call(
        kernel,
        out_shape=(
            jax.ShapeDtypeStruct((tok, rows * X), BF16),
            jax.ShapeDtypeStruct((rows, hid), F32),
            jax.ShapeDtypeStruct((n, rows, hid), BF16),
        ),
        in_specs=[anywhere, vmem, vmem, vmem, anywhere, anywhere],
        out_specs=[anywhere] * 3,
        scratch_shapes=[
            pltpu.VMEM((tok, rows * X), BF16),
            pltpu.VMEM((rows, hid), F32),
            pltpu.VMEM((n, rows, hid), BF16),
            pltpu.VMEM((rows, hid), F32),
            pltpu.VMEM((rows, hid), F32),
            pltpu.VMEM((n, tok, rows), BF16),
            pltpu.VMEM((n, rows, hid), BF16),
            pltpu.VMEM((T, X, rows, hid), BF16),
            pltpu.VMEM((T, tok, hid), BF16),
            pltpu.VMEM((hid, tok), BF16),
            pltpu.VMEM((n, hid, rows), BF16),
            pltpu.VMEM((Z, G_SPLIT, rows), BF16),
            *[pltpu.VMEM((Z - 1, G_SPLIT, rows), BF16)] * 4,
            *[pltpu.VMEM((Z - 1, X, gb, rows), BF16)] * 4,
            pltpu.VMEM((X, gb, rows), F32),
            pltpu.VMEM((2, gb, rows), BF16),
            pltpu.VMEM((hid, rows), F32),
            dma((tok // 256 + Z,)), dma((2,)), dma((n,)), dma((T - 1,)), dma((T - 1,)),
            dma((Z * X * 2,)), dma((T * X * 2,)),
            dma((2, 17)), dma((2, 17)),
            dma((Z,)), dma((Z,)),
            dma((6,)), dma((6,)), dma((6,)), dma((6,)),
            dma(()), dma(()),
        ],
        compiler_params=pltpu.CompilerParams(
            collective_id=0, has_side_effects=True, vmem_limit_bytes=60 * 1024 * 1024
        ),
        cost_estimate=pl.CostEstimate(
            flops=4 * tok * rows * n * hid, bytes_accessed=2 * tok * rows * n * 2, transcendentals=tok * hid
        ),
    )(inputs, pre_act, grad_hidden, master, moment_one, moment_two)
    new_master, new_one, new_two = adam(grad, master, moment_one, moment_two)
    return (grad_input, new_master, new_one, new_two, new_weights.reshape(n * rows, hid))


def local_plain(inputs, pre_act, grad_hidden, master, moment_one, moment_two):
    act_grad = (grad_hidden.astype(F32) * gelu_slope(pre_act.astype(F32))).astype(BF16)
    weights = lax.all_gather(master.astype(BF16), "dp", axis=0, tiled=True)
    rows = lax.all_to_all(weights, "tensor", split_axis=0, concat_axis=1, tiled=True)
    acts = lax.all_gather(act_grad, "tensor", axis=1, tiled=True)
    grad_input = jnp.einsum("th,dh->td", acts, rows, preferred_element_type=F32).astype(BF16)
    term = jnp.einsum("tr,th->rh", inputs, act_grad, preferred_element_type=F32)
    codes, scale = encode(term)
    grad = lax.psum_scatter(decode(codes, scale), "dp", scatter_dimension=0, tiled=True)
    new_master, new_one, new_two = adam(grad, master, moment_one, moment_two)
    new_weights = lax.all_gather(new_master.astype(BF16), "dp", axis=0, tiled=True)
    return (grad_input, new_master, new_one, new_two, new_weights)


def solution(mesh):
    sizes = dict(mesh.shape)
    body = local_kernel if sizes == {"dp": Z * X, "tensor": T} else local_plain
    two = P("dp", "tensor")
    return jax.shard_map(
        body,
        mesh=mesh,
        in_specs=(P("dp", None), two, two, two, two, two),
        out_specs=(two, two, two, two, P(None, "tensor")),
        check_vma=False,
    )
```

```python
import functools
import math

import jax
import jax.numpy as jnp
from jax import lax
from jax.experimental import pallas as pl
from jax.experimental.pallas import tpu as pltpu
from jax.sharding import PartitionSpec as P

QBLOCK = 256
ADAM_STEP = 10
Z, X, T = 4, 2, 4
W_SPLIT = 464
G_SPLIT = 160
N_SPLIT = 320
PIECES = 4
MESH = pl.DeviceIdType.MESH
F32, BF16 = jnp.float32, jnp.bfloat16


def gelu_slope(value):
    cdf = 0.5 * (1.0 + lax.erf(value * (1.0 / math.sqrt(2.0))))
    pdf = jnp.exp(-0.5 * value * value) / math.sqrt(2.0 * math.pi)
    return cdf + value * pdf


def encode(term):
    rows, cols = term.shape
    blocks = term.reshape(rows, cols // QBLOCK, QBLOCK)
    scale = (jnp.max(jnp.abs(blocks), axis=2) + 1e-06) / 127.0
    codes = jnp.clip(blocks / scale[:, :, None], -127.0, 127.0).astype(BF16)
    return (codes.reshape(rows, cols), scale)


def decode(codes, scale):
    rows, cols = codes.shape
    blocks = codes.astype(F32).reshape(rows, cols // QBLOCK, QBLOCK)
    return (blocks * scale[:, :, None]).reshape(rows, cols)


def adam(grad, master, moment_one, moment_two):
    new_one = 0.9 * moment_one + 0.1 * grad
    new_two = 0.999 * moment_two + 0.001 * grad * grad
    corr_one = 1.0 - 0.9**ADAM_STEP
    corr_two = 1.0 - 0.999**ADAM_STEP
    update = new_one / corr_one / (jnp.sqrt(new_two / corr_two) + 1e-08) + 0.01 * master
    return master - 0.01 * update, new_one, new_two


def kernel(
    in_hbm, pre_ref, hid_ref, master_ref, one_hbm, two_hbm,
    gi_hbm, nm_hbm, n1_hbm, n2_hbm, nw_hbm,
    gi_ref, nm_ref, n1_ref, n2_ref, nw_ref, one_ref, two_ref,
    xin, w_buf, wx, act, act_t, term, xr, zua, zda, sua, sda, zub, zdb, sub, sdb, fxs, fxr, grad_t,
    out_sem, mom_sem, in_sem, act_s, act_r, ws, wr, wag, nag, mag, rxs, rxr, ras, rar, rbs, rbr, fs, fr,
):
    r = lax.axis_index("dp")
    k = lax.axis_index("tensor")
    z, x = r // X, r % X
    o = 1 - x
    across, above, below = {"dp": r + 1 - 2 * x}, {"dp": r + X}, {"dp": r - X}
    up_ok, dn_ok = z <= Z - 2, z >= 1
    tok, hid = pre_ref.shape
    rows = master_ref.shape[0]
    pend = []

    def when(cond, fn):
        if cond is None:
            fn()
        else:
            pl.when(cond)(fn)

    def rc(src, dst, ssem, rsem, dev):
        return pltpu.make_async_remote_copy(
            src_ref=src, dst_ref=dst, send_sem=ssem, recv_sem=rsem, device_id=dev, device_id_type=MESH
        )

    def send(cond, make):
        when(cond, lambda: make().start())
        pend.append((cond, make))

    def got(cond, make):
        when(cond, lambda: make().wait_recv())

    class Gather:
        def __init__(self, buf, sems, first, split, end, on_block, late):
            self.buf, self.s, self.on = buf, sems, on_block
            self.rows_a, self.rows_b = pl.ds(first, split - first), pl.ds(split, end - split)
            self.late, self.kept = late, []

        def a(self, zz, xx):
            return self.buf.at[X * zz + xx, self.rows_a, :]

        def b(self, zz):
            return self.buf.at[pl.ds(X * zz, X), self.rows_b, :]

        def b1(self, zz, xx):
            return self.buf.at[X * zz + xx, self.rows_b, :]

        def mk(self, ref, idx, dev):
            return lambda: rc(ref(), ref(), self.s.at[0, idx], self.s.at[1, idx], dev)

        def za(self, s):
            zz_u, zz_d = z - s, z + s
            send(up_ok & (zz_u >= 0), self.mk(lambda: self.a(zz_u, x), s, above))
            send(dn_ok & (zz_d <= Z - 1), self.mk(lambda: self.a(zz_d, x), 3 + s, below))

        def zb(self, s):
            zz_u, zz_d = z - s, z + s
            send(up_ok & (zz_u >= 0), self.mk(lambda: self.b(zz_u), 6 + s, above))
            send(dn_ok & (zz_d <= Z - 1), self.mk(lambda: self.b(zz_d), 9 + s, below))

        def xa(self, cond, zz):
            if self.late:
                self.kept.append((cond, zz))
            else:
                self.xa_now(cond, zz)

        def flush(self):
            for cond, zz in self.kept:
                self.xa_now(cond, zz)
            self.kept = []

        def xa_now(self, cond, zz):
            send(cond, self.mk(lambda: self.a(zz, x), 12 + zz, across))

        def start(self):
            self.xa(None, z)
            self.za(0)
            send(None, self.mk(lambda: self.b1(z, x), 16, across))
            self.on(None, z, x, 0)

        def part_a(self, s):
            zu, zd = z - 1 - s, z + 1 + s
            cu, cd = zu >= 0, zd <= Z - 1
            got(cu, self.mk(lambda: self.a(zu, x), s, above))
            got(cd, self.mk(lambda: self.a(zd, x), 3 + s, below))
            if s + 1 < Z - 1:
                self.za(s + 1)
            self.xa(cu, zu)
            self.xa(cd, zd)
            self.on(cu, zu, x, 0)
            self.on(cd, zd, x, 0)

        def part_b(self, s):
            if s == 0:
                got(None, self.mk(lambda: self.b1(z, o), 16, across))
            else:
                zu, zd = z - s, z + s
                cu, cd = zu >= 0, zd <= Z - 1
                got(cu, self.mk(lambda: self.b(zu), 6 + s - 1, above))
                got(cd, self.mk(lambda: self.b(zd), 9 + s - 1, below))
            if s < Z - 1:
                self.zb(s)
            if s == 0:
                for xx in range(X):
                    self.on(None, z, xx, 1)
            else:
                for xx in range(X):
                    self.on(cu, zu, xx, 1)
                    self.on(cd, zd, xx, 1)

        def finish_x(self, *only):
            for j in only or range(Z):
                zz = (z + j) % Z
                got(None, self.mk(lambda: self.a(zz, o), 12 + zz, across))
                self.on(None, zz, o, 0)

    def w_part(ref, idx, xx, part):
        lo, n = (0, W_SPLIT) if part == 0 else (W_SPLIT, rows - W_SPLIT)
        return ref.at[idx, xx, pl.ds(lo, n), :]

    def to_tensor(cond, zz, xx, part):
        lo, n = (0, W_SPLIT) if part == 0 else (W_SPLIT, rows - W_SPLIT)
        sem = (zz * X + xx) * 2 + part
        rsem = (k * X + xx) * 2 + part
        c = zz != k
        send(
            c if cond is None else cond & c,
            lambda: rc(
                w_buf.at[X * zz + xx, pl.ds(lo, n), :], w_part(wx, k, xx, part),
                ws.at[sem], wr.at[rsem], {"tensor": zz},
            ),
        )

    half = rows // 2
    gw = Gather(w_buf, wag, 0, W_SPLIT, rows, to_tensor, True)
    gn, gm = [
        Gather(nw_ref, sems, i * half, i * half + N_SPLIT, (i + 1) * half, lambda *_: None, False)
        for i, sems in enumerate((nag, mag))
    ]

    hi = z // 2
    order = [3 - 3 * hi, 2 - hi, 1 - z + 4 * hi, z]

    def fetch(j):
        blk = X * order[j // 2] + (o if j % 2 == 0 else x)
        col = pl.multiple_of(blk * rows, 128)
        return pltpu.make_async_copy(in_hbm.at[:, pl.ds(col, rows)], xin.at[j], in_sem.at[j])

    for j in range(Z * X):
        fetch(j).start()
    moments = [
        pltpu.make_async_copy(one_hbm, one_ref, mom_sem.at[0]),
        pltpu.make_async_copy(two_hbm, two_ref, mom_sem.at[1]),
    ]
    for c in moments:
        c.start()
    w_buf[r] = master_ref[...].astype(BF16)

    barrier = pltpu.get_barrier_semaphore()

    def hello(dev):
        pl.semaphore_signal(barrier, inc=1, device_id=dev, device_id_type=MESH)

    hello(across)
    when(up_ok, lambda: hello(above))
    when(dn_ok, lambda: hello(below))
    for j in range(1, T):
        hello({"tensor": (k + j) % T})
    pl.semaphore_wait(barrier, T + 1 + z * (Z - 1 - z) // 2)

    gw.start()

    step_t = 256

    @pl.loop(0, tok // step_t)
    def _(i):
        here = pl.ds(pl.multiple_of(i * step_t, step_t), step_t)
        val = hid_ref[here, :].astype(F32) * gelu_slope(pre_ref[here, :].astype(F32))
        act[k, here, :] = val.astype(BF16)
        act_t[:, here] = val.T.astype(BF16)

    def make_term(j):
        blk = X * order[j // 2] + (o if j % 2 == 0 else x)
        fetch(j).wait()

        @pl.loop(0, rows // 256)
        def _(c):
            cols = pl.ds(pl.multiple_of(c * 256, 256), 256)
            t = jnp.dot(act_t[...], xin[j, :, cols], preferred_element_type=F32)
            scale = (jnp.max(jnp.abs(t), axis=0, keepdims=True) + 1e-06) / 127.0
            codes = jnp.clip(t / scale, -127.0, 127.0).astype(BF16)
            term[blk, :, cols] = (codes.astype(F32) * scale).astype(BF16)

    def xr_copy(t, own):
        return lambda: rc(
            term.at[X * t + own, pl.ds(0, G_SPLIT), :], xr.at[t], rxs.at[t], rxr.at[t], across
        )

    for i in range(Z):
        make_term(2 * i)
        send(None, xr_copy(order[i], o))
        make_term(2 * i + 1)
        if i == 0:
            for j in range(1, T):
                kk = (k + j) % T
                send(
                    None,
                    lambda kk=kk, j=j: rc(
                        act.at[k], act.at[k], act_s.at[j - 1], act_r.at[j - 1], {"tensor": kk}
                    ),
                )

    def z_sum(s, value, arrived, zu, zd, su, sd, ssem, rsem):
        tu, td = z + 3 - s, z - 3 + s
        cu, cd = up_ok & (z <= s), dn_ok & (z >= 3 - s)
        for cond, edge, t, zin, out, base, dev in (
            (cu, z == 0, tu, zu, su, 0, above),
            (cd, z == Z - 1, td, zd, sd, 3, below),
        ):
            make = lambda zin=zin, out=out, base=base, dev=dev: rc(
                out.at[s], zin.at[s], ssem.at[base + s], rsem.at[base + s], dev
            )
            def body(edge=edge, t=t, zin=zin, out=out, base=base, dev=dev, make=make):
                arrived(t)
                own = value(t)

                @pl.when(edge)
                def _():
                    out[s] = own().astype(BF16)

                if s > 0:
                    @pl.when(jnp.logical_not(edge))
                    def _():
                        rc(out.at[s], zin.at[s - 1], ssem.at[base + s - 1], rsem.at[base + s - 1], dev).wait_recv()
                        out[s] = (own() + zin[s - 1].astype(F32)).astype(BF16)

            pl.when(cond)(body)
            send(cond, make)

    def value_a(t):
        return lambda: term[X * t + x, :G_SPLIT, :].astype(F32) + xr[t].astype(F32)

    def value_b(t):
        return lambda: term[pl.ds(X * t, X), G_SPLIT:, :].astype(F32)

    def arrived_a(t):
        xr_copy(t, o)().wait_recv()

    def sum_a(s):
        z_sum(s, value_a, arrived_a, zua, zda, sua, sda, ras, rar)

    def sum_b(s):
        z_sum(s, value_b, lambda t: None, zub, zdb, sub, sdb, rbs, rbr)

    sum_b(0)
    gw.part_b(0)
    for s in range(Z - 1):
        sum_a(s)
        if s == 1:
            gw.flush()
        gw.part_a(s)
        if s + 1 < Z - 1:
            sum_b(s + 1)
        gw.part_b(s + 1)

    last = Z - 2
    sb = fxs
    sb[...] = term[pl.ds(X * z, X), G_SPLIT:, :].astype(F32)
    for cond, zin, base, dev in ((dn_ok, zub, 0, above), (up_ok, zdb, 3, below)):
        def body(zin=zin, base=base, dev=dev):
            rc(zin.at[last], zin.at[last], rbs.at[base + last], rbr.at[base + last], dev).wait_recv()
            sb[...] += zin[last].astype(F32)
        pl.when(cond)(body)
    fxr[0] = sb[o].astype(BF16)
    fx = lambda: rc(fxr.at[0], fxr.at[1], fs, fr, across)
    send(None, fx)
    arrived_a(z)
    grad_t[:G_SPLIT, :] = value_a(z)()
    for cond, zin, base, dev in ((dn_ok, zua, 0, above), (up_ok, zda, 3, below)):
        def body(zin=zin, base=base, dev=dev):
            rc(zin.at[last], zin.at[last], ras.at[base + last], rar.at[base + last], dev).wait_recv()
            grad_t[:G_SPLIT, :] += zin[last].astype(F32)
        pl.when(cond)(body)
    fx().wait_recv()
    gw.flush()
    grad_t[G_SPLIT:, :] = sb[x] + fxr[1].astype(F32)

    for c in moments:
        c.wait()

    for g, part in ((gn, 0), (gm, 1)):
        @pl.loop(0, half // 128)
        def _(c, part=part):
            here = pl.ds(pl.multiple_of(part * half + c * 128, 128), 128)
            nm, n1, n2 = adam(
                grad_t[:, here].T, master_ref[here, :], one_ref[here, :], two_ref[here, :]
            )
            nm_ref[here, :] = nm
            n1_ref[here, :] = n1
            n2_ref[here, :] = n2
            nw_ref[r, here, :] = nm.astype(BF16)

        g.start()

    writes = []

    def write(src, dst):
        c = pltpu.make_async_copy(src, dst, out_sem.at[len(writes)])
        c.start()
        writes.append(c)

    write(nm_ref, nm_hbm)
    write(n1_ref, n1_hbm)
    write(n2_ref, n2_hbm)
    for s in range(Z - 1):
        gn.part_a(s)
        gm.part_a(s)
        gn.part_b(s)
        gm.part_b(s)
        if s == 1:
            gw.finish_x()
    gn.part_b(Z - 1)
    gm.part_b(Z - 1)

    wx[k] = w_buf[pl.ds(X * k, X)]
    for j in range(1, T):
        src = (k + T - j) % T
        got(None, lambda: rc(act.at[src], act.at[src], act_s.at[j - 1], act_r.at[j - 1], {"tensor": src}))
        for xx in range(X):
            for part in range(2):
                got(
                    None,
                    lambda: rc(
                        w_part(wx, src, xx, part), w_part(wx, src, xx, part),
                        ws.at[0], wr.at[(src * X + xx) * 2 + part], {"tensor": src},
                    ),
                )

    for i in range(tok // step_t):
        here = pl.ds(i * step_t, step_t)
        for xx in range(X):
            total = None
            for src in range(T):
                part = lax.dot_general(
                    act[src, here, :], wx[src, xx], (((1,), (1,)), ((), ())), preferred_element_type=F32
                )
                total = part if total is None else total + part
            gi_ref[here, xx * rows:(xx + 1) * rows] = total.astype(BF16)
        write(gi_ref.at[here, :], gi_hbm.at[here, :])

    for j in range(Z):
        gn.finish_x(j)
        gm.finish_x(j)
        both = pl.ds(X * ((z + j) % Z), X)
        write(nw_ref.at[both], nw_hbm.at[both])
    for c in writes:
        c.wait()
    for cond, make in pend:
        when(cond, lambda: make().wait_send())


def place(*refs):
    srcs, dsts, sems = refs[:5], refs[5:10], refs[10]
    copies = []
    for src, dst in zip(srcs, dsts):
        step = src.shape[0] // PIECES
        for i in range(PIECES):
            here = pl.ds(i * step, step)
            copies.append(pltpu.make_async_copy(src.at[here], dst.at[here], sems.at[len(copies)]))
    for c in copies:
        c.start()
    for c in copies:
        c.wait()


def local_kernel(inputs, pre_act, grad_hidden, master, moment_one, moment_two):
    tok, hid = pre_act.shape
    rows = master.shape[0]
    n = Z * X
    gb = hid - G_SPLIT
    vmem = pl.BlockSpec(memory_space=pltpu.VMEM)
    dma = pltpu.SemaphoreType.DMA
    anywhere, hbm = pl.BlockSpec(memory_space=pl.ANY), pl.BlockSpec(memory_space=pltpu.HBM)
    out = pl.pallas_call(
        kernel,
        out_shape=(
            jax.ShapeDtypeStruct((tok, rows * X), BF16),
            *[jax.ShapeDtypeStruct((rows, hid), F32)] * 3,
            jax.ShapeDtypeStruct((n, rows, hid), BF16),
        ),
        in_specs=[anywhere, vmem, vmem, vmem, anywhere, anywhere],
        out_specs=[anywhere] * 5,
        scratch_shapes=[
            pltpu.VMEM((tok, rows * X), BF16),
            *[pltpu.VMEM((rows, hid), F32)] * 3,
            pltpu.VMEM((n, rows, hid), BF16),
            pltpu.VMEM((rows, hid), F32),
            pltpu.VMEM((rows, hid), F32),
            pltpu.VMEM((n, tok, rows), BF16),
            pltpu.VMEM((n, rows, hid), BF16),
            pltpu.VMEM((T, X, rows, hid), BF16),
            pltpu.VMEM((T, tok, hid), BF16),
            pltpu.VMEM((hid, tok), BF16),
            pltpu.VMEM((n, hid, rows), BF16),
            pltpu.VMEM((Z, G_SPLIT, rows), BF16),
            *[pltpu.VMEM((Z - 1, G_SPLIT, rows), BF16)] * 4,
            *[pltpu.VMEM((Z - 1, X, gb, rows), BF16)] * 4,
            pltpu.VMEM((X, gb, rows), F32),
            pltpu.VMEM((2, gb, rows), BF16),
            pltpu.VMEM((hid, rows), F32),
            dma((tok // 256 + Z + 3,)), dma((2,)), dma((n,)), dma((T - 1,)), dma((T - 1,)),
            dma((Z * X * 2,)), dma((T * X * 2,)),
            dma((2, 17)), dma((2, 17)), dma((2, 17)),
            dma((Z,)), dma((Z,)),
            dma((6,)), dma((6,)), dma((6,)), dma((6,)),
            dma(()), dma(()),
        ],
        compiler_params=pltpu.CompilerParams(
            collective_id=0, has_side_effects=True, vmem_limit_bytes=60 * 1024 * 1024
        ),
        cost_estimate=pl.CostEstimate(
            flops=4 * tok * rows * n * hid, bytes_accessed=2 * tok * rows * n * 2, transcendentals=tok * hid
        ),
    )(inputs, pre_act, grad_hidden, master, moment_one, moment_two)
    out = pl.pallas_call(
        place,
        out_shape=tuple(jax.ShapeDtypeStruct(a.shape, a.dtype) for a in out),
        in_specs=[hbm] * 5,
        out_specs=[hbm] * 5,
        scratch_shapes=[dma((5 * PIECES,))],
        compiler_params=pltpu.CompilerParams(vmem_limit_bytes=60 * 1024 * 1024),
        cost_estimate=pl.CostEstimate(flops=0, bytes_accessed=2 * 9 * 2**20, transcendentals=0),
    )(*out)
    return (*out[:4], out[4].reshape(n * rows, hid))


def local_plain(inputs, pre_act, grad_hidden, master, moment_one, moment_two):
    act_grad = (grad_hidden.astype(F32) * gelu_slope(pre_act.astype(F32))).astype(BF16)
    weights = lax.all_gather(master.astype(BF16), "dp", axis=0, tiled=True)
    rows = lax.all_to_all(weights, "tensor", split_axis=0, concat_axis=1, tiled=True)
    acts = lax.all_gather(act_grad, "tensor", axis=1, tiled=True)
    grad_input = jnp.einsum("th,dh->td", acts, rows, preferred_element_type=F32).astype(BF16)
    term = jnp.einsum("tr,th->rh", inputs, act_grad, preferred_element_type=F32)
    codes, scale = encode(term)
    grad = lax.psum_scatter(decode(codes, scale), "dp", scatter_dimension=0, tiled=True)
    new_master, new_one, new_two = adam(grad, master, moment_one, moment_two)
    new_weights = lax.all_gather(new_master.astype(BF16), "dp", axis=0, tiled=True)
    return (grad_input, new_master, new_one, new_two, new_weights)


def solution(mesh):
    sizes = dict(mesh.shape)
    body = local_kernel if sizes == {"dp": Z * X, "tensor": T} else local_plain
    two = P("dp", "tensor")
    return jax.shard_map(
        body,
        mesh=mesh,
        in_specs=(P("dp", None), two, two, two, two, two),
        out_specs=(two, two, two, two, P(None, "tensor")),
        check_vma=False,
    )
```

```python
import functools
import math

import jax
import jax.numpy as jnp
from jax import lax
from jax.experimental import pallas as pl
from jax.experimental.pallas import tpu as pltpu
from jax.sharding import PartitionSpec as P

QBLOCK = 256
ADAM_STEP = 10
Z, X, T = 4, 2, 4
W_SPLIT = 464
G_SPLIT = 160
N_SPLIT = 352
PIECES = 4
MESH = pl.DeviceIdType.MESH
F32, BF16 = jnp.float32, jnp.bfloat16


def gelu_slope(value):
    cdf = 0.5 * (1.0 + lax.erf(value * (1.0 / math.sqrt(2.0))))
    pdf = jnp.exp(-0.5 * value * value) / math.sqrt(2.0 * math.pi)
    return cdf + value * pdf


def encode(term):
    rows, cols = term.shape
    blocks = term.reshape(rows, cols // QBLOCK, QBLOCK)
    scale = (jnp.max(jnp.abs(blocks), axis=2) + 1e-06) / 127.0
    codes = jnp.clip(blocks / scale[:, :, None], -127.0, 127.0).astype(BF16)
    return (codes.reshape(rows, cols), scale)


def decode(codes, scale):
    rows, cols = codes.shape
    blocks = codes.astype(F32).reshape(rows, cols // QBLOCK, QBLOCK)
    return (blocks * scale[:, :, None]).reshape(rows, cols)


def adam(grad, master, moment_one, moment_two):
    new_one = 0.9 * moment_one + 0.1 * grad
    new_two = 0.999 * moment_two + 0.001 * grad * grad
    corr_one = 1.0 - 0.9**ADAM_STEP
    corr_two = 1.0 - 0.999**ADAM_STEP
    update = new_one / corr_one / (jnp.sqrt(new_two / corr_two) + 1e-08) + 0.01 * master
    return master - 0.01 * update, new_one, new_two


def kernel(
    in_hbm, pre_ref, hid_ref, master_ref, one_hbm, two_hbm,
    gi_hbm, nm_hbm, n1_hbm, n2_hbm, nw_hbm,
    gi_ref, nm_ref, n1_ref, n2_ref, nw_ref, one_ref, two_ref,
    xin, w_buf, wx, act, act_t, term, xr, zua, zda, sua, sda, zub, zdb, sub, sdb, fxs, fxr, grad_t,
    out_sem, mom_sem, in_sem, act_s, act_r, ws, wr, wag, nag, mag, rxs, rxr, ras, rar, rbs, rbr, fs, fr,
):
    r = lax.axis_index("dp")
    k = lax.axis_index("tensor")
    z, x = r // X, r % X
    o = 1 - x
    across, above, below = {"dp": r + 1 - 2 * x}, {"dp": r + X}, {"dp": r - X}
    up_ok, dn_ok = z <= Z - 2, z >= 1
    tok, hid = pre_ref.shape
    rows = master_ref.shape[0]
    pend = []

    def when(cond, fn):
        if cond is None:
            fn()
        else:
            pl.when(cond)(fn)

    def rc(src, dst, ssem, rsem, dev):
        return pltpu.make_async_remote_copy(
            src_ref=src, dst_ref=dst, send_sem=ssem, recv_sem=rsem, device_id=dev, device_id_type=MESH
        )

    def send(cond, make):
        when(cond, lambda: make().start())
        pend.append((cond, make))

    def got(cond, make):
        when(cond, lambda: make().wait_recv())

    class Gather:
        def __init__(self, buf, sems, first, split, end, on_block, late):
            self.buf, self.s, self.on = buf, sems, on_block
            self.rows_a, self.rows_b = pl.ds(first, split - first), pl.ds(split, end - split)
            self.late, self.kept = late, []

        def a(self, zz, xx):
            return self.buf.at[X * zz + xx, self.rows_a, :]

        def b(self, zz):
            return self.buf.at[pl.ds(X * zz, X), self.rows_b, :]

        def b1(self, zz, xx):
            return self.buf.at[X * zz + xx, self.rows_b, :]

        def mk(self, ref, idx, dev):
            return lambda: rc(ref(), ref(), self.s.at[0, idx], self.s.at[1, idx], dev)

        def za(self, s):
            zz_u, zz_d = z - s, z + s
            send(up_ok & (zz_u >= 0), self.mk(lambda: self.a(zz_u, x), s, above))
            send(dn_ok & (zz_d <= Z - 1), self.mk(lambda: self.a(zz_d, x), 3 + s, below))

        def zb(self, s):
            zz_u, zz_d = z - s, z + s
            send(up_ok & (zz_u >= 0), self.mk(lambda: self.b(zz_u), 6 + s, above))
            send(dn_ok & (zz_d <= Z - 1), self.mk(lambda: self.b(zz_d), 9 + s, below))

        def xa(self, cond, zz):
            if self.late:
                self.kept.append((cond, zz))
            else:
                self.xa_now(cond, zz)

        def flush(self):
            for cond, zz in self.kept:
                self.xa_now(cond, zz)
            self.kept = []

        def xa_now(self, cond, zz):
            send(cond, self.mk(lambda: self.a(zz, x), 12 + zz, across))

        def start(self):
            self.xa(None, z)
            self.za(0)
            send(None, self.mk(lambda: self.b1(z, x), 16, across))
            self.on(None, z, x, 0)

        def part_a(self, s):
            zu, zd = z - 1 - s, z + 1 + s
            cu, cd = zu >= 0, zd <= Z - 1
            got(cu, self.mk(lambda: self.a(zu, x), s, above))
            got(cd, self.mk(lambda: self.a(zd, x), 3 + s, below))
            if s + 1 < Z - 1:
                self.za(s + 1)
            self.xa(cu, zu)
            self.xa(cd, zd)
            self.on(cu, zu, x, 0)
            self.on(cd, zd, x, 0)

        def part_b(self, s):
            if s == 0:
                got(None, self.mk(lambda: self.b1(z, o), 16, across))
            else:
                zu, zd = z - s, z + s
                cu, cd = zu >= 0, zd <= Z - 1
                got(cu, self.mk(lambda: self.b(zu), 6 + s - 1, above))
                got(cd, self.mk(lambda: self.b(zd), 9 + s - 1, below))
            if s < Z - 1:
                self.zb(s)
            if s == 0:
                for xx in range(X):
                    self.on(None, z, xx, 1)
            else:
                for xx in range(X):
                    self.on(cu, zu, xx, 1)
                    self.on(cd, zd, xx, 1)

        def finish_x(self, *only):
            for j in only or range(Z):
                zz = (z + j) % Z
                got(None, self.mk(lambda: self.a(zz, o), 12 + zz, across))
                self.on(None, zz, o, 0)

    def w_part(ref, idx, xx, part):
        lo, n = (0, W_SPLIT) if part == 0 else (W_SPLIT, rows - W_SPLIT)
        return ref.at[idx, xx, pl.ds(lo, n), :]

    def to_tensor(cond, zz, xx, part):
        lo, n = (0, W_SPLIT) if part == 0 else (W_SPLIT, rows - W_SPLIT)
        sem = (zz * X + xx) * 2 + part
        rsem = (k * X + xx) * 2 + part
        c = zz != k
        send(
            c if cond is None else cond & c,
            lambda: rc(
                w_buf.at[X * zz + xx, pl.ds(lo, n), :], w_part(wx, k, xx, part),
                ws.at[sem], wr.at[rsem], {"tensor": zz},
            ),
        )

    half = rows // 2
    gw = Gather(w_buf, wag, 0, W_SPLIT, rows, to_tensor, False)
    gn, gm = [
        Gather(nw_ref, sems, i * half, i * half + N_SPLIT, (i + 1) * half, lambda *_: None, False)
        for i, sems in enumerate((nag, mag))
    ]

    hi = z // 2
    order = [3 - 3 * hi, 2 - hi, 1 - z + 4 * hi, z]

    def fetch(j):
        blk = X * order[j // 2] + (o if j % 2 == 0 else x)
        col = pl.multiple_of(blk * rows, 128)
        return pltpu.make_async_copy(in_hbm.at[:, pl.ds(col, rows)], xin.at[j], in_sem.at[j])

    for j in range(Z * X):
        fetch(j).start()
    moments = [
        pltpu.make_async_copy(one_hbm, one_ref, mom_sem.at[0]),
        pltpu.make_async_copy(two_hbm, two_ref, mom_sem.at[1]),
    ]
    for c in moments:
        c.start()
    w_buf[r] = master_ref[...].astype(BF16)

    barrier = pltpu.get_barrier_semaphore()

    def hello(dev):
        pl.semaphore_signal(barrier, inc=1, device_id=dev, device_id_type=MESH)

    hello(across)
    when(up_ok, lambda: hello(above))
    when(dn_ok, lambda: hello(below))
    for j in range(1, T):
        hello({"tensor": (k + j) % T})
    pl.semaphore_wait(barrier, T + 1 + z * (Z - 1 - z) // 2)

    gw.start()

    step_t = 256

    @pl.loop(0, tok // step_t)
    def _(i):
        here = pl.ds(pl.multiple_of(i * step_t, step_t), step_t)
        val = hid_ref[here, :].astype(F32) * gelu_slope(pre_ref[here, :].astype(F32))
        act[k, here, :] = val.astype(BF16)
        act_t[:, here] = val.T.astype(BF16)

    def make_term(h, j):
        blk = X * order[j // 2] + (o if j % 2 == 0 else x)
        if h == 0:
            fetch(j).wait()

        @pl.loop(0, half // 128)
        def _(c):
            at = pl.multiple_of(c * 128, 128)
            cols = pl.ds(h * half + at, 128)
            t = jnp.dot(act_t[...], xin[j, :, cols], preferred_element_type=F32)
            scale = (jnp.max(jnp.abs(t), axis=0, keepdims=True) + 1e-06) / 127.0
            codes = jnp.clip(t / scale, -127.0, 127.0).astype(BF16)
            term[h, blk, :, pl.ds(at, 128)] = (codes.astype(F32) * scale).astype(BF16)

    def xr_copy(h, t, own):
        return lambda: rc(
            term.at[h, X * t + own, pl.ds(0, G_SPLIT), :], xr.at[h, t], rxs.at[h, t], rxr.at[h, t], across
        )

    for h in range(2):
        for i in range(Z):
            make_term(h, 2 * i)
            send(None, xr_copy(h, order[i], o))
            make_term(h, 2 * i + 1)
        if h == 0:
            for j in range(1, T):
                kk = (k + j) % T
                send(
                    None,
                    lambda kk=kk, j=j: rc(
                        act.at[k], act.at[k], act_s.at[j - 1], act_r.at[j - 1], {"tensor": kk}
                    ),
                )

    def z_sum(s, value, arrived, zu, zd, su, sd, ssem, rsem):
        tu, td = z + 3 - s, z - 3 + s
        cu, cd = up_ok & (z <= s), dn_ok & (z >= 3 - s)
        for cond, edge, t, zin, out, base, dev in (
            (cu, z == 0, tu, zu, su, 0, above),
            (cd, z == Z - 1, td, zd, sd, 3, below),
        ):
            make = lambda zin=zin, out=out, base=base, dev=dev: rc(
                out.at[s], zin.at[s], ssem.at[base + s], rsem.at[base + s], dev
            )
            def body(edge=edge, t=t, zin=zin, out=out, base=base, dev=dev, make=make):
                arrived(t)
                own = value(t)

                @pl.when(edge)
                def _():
                    out[s] = own().astype(BF16)

                if s > 0:
                    @pl.when(jnp.logical_not(edge))
                    def _():
                        rc(out.at[s], zin.at[s - 1], ssem.at[base + s - 1], rsem.at[base + s - 1], dev).wait_recv()
                        out[s] = (own() + zin[s - 1].astype(F32)).astype(BF16)

            pl.when(cond)(body)
            send(cond, make)

    def value_a(h, t):
        return lambda: term[h, X * t + x, :G_SPLIT, :].astype(F32) + xr[h, t].astype(F32)

    def value_b(h, t):
        return lambda: term[h, pl.ds(X * t, X), G_SPLIT:, :].astype(F32)

    def arrived_a(h, t):
        xr_copy(h, t, o)().wait_recv()

    def sum_a(h, s):
        z_sum(
            s, lambda t: value_a(h, t), lambda t: arrived_a(h, t),
            zua.at[h], zda.at[h], sua.at[h], sda.at[h], ras.at[h], rar.at[h],
        )

    def sum_b(h, s):
        z_sum(
            s, lambda t: value_b(h, t), lambda t: None,
            zub.at[h], zdb.at[h], sub.at[h], sdb.at[h], rbs.at[h], rbr.at[h],
        )

    last = Z - 2

    def final_sum(h):
        sb, ga = fxs.at[h], grad_t.at[h, pl.ds(0, G_SPLIT), :]
        sb[...] = value_b(h, z)()
        for cond, zin, base, dev in ((dn_ok, zub, 0, above), (up_ok, zdb, 3, below)):
            def body(zin=zin, base=base, dev=dev):
                slot = zin.at[h, last]
                rc(slot, slot, rbs.at[h, base + last], rbr.at[h, base + last], dev).wait_recv()
                sb[...] += slot[...].astype(F32)
            pl.when(cond)(body)
        fxr[h, 0] = sb[o].astype(BF16)
        fx = lambda: rc(fxr.at[h, 0], fxr.at[h, 1], fs.at[h], fr.at[h], across)
        send(None, fx)
        arrived_a(h, z)
        ga[...] = value_a(h, z)()
        for cond, zin, base, dev in ((dn_ok, zua, 0, above), (up_ok, zda, 3, below)):
            def body(zin=zin, base=base, dev=dev):
                slot = zin.at[h, last]
                rc(slot, slot, ras.at[h, base + last], rar.at[h, base + last], dev).wait_recv()
                ga[...] += slot[...].astype(F32)
            pl.when(cond)(body)
        fx().wait_recv()
        grad_t[h, G_SPLIT:, :] = sb[x] + fxr[h, 1].astype(F32)

    def step_adam(h):
        @pl.loop(0, half // 128)
        def _(c):
            at = pl.multiple_of(c * 128, 128)
            here = pl.ds(h * half + at, 128)
            nm, n1, n2 = adam(
                grad_t[h, :, pl.ds(at, 128)].T, master_ref[here, :], one_ref[here, :], two_ref[here, :]
            )
            nm_ref[here, :] = nm
            n1_ref[here, :] = n1
            n2_ref[here, :] = n2
            nw_ref[r, here, :] = nm.astype(BF16)

    sum_b(0, 0)
    gw.part_b(0)
    sum_a(0, 0)
    gw.part_a(0)
    sum_b(0, 1)
    sum_a(0, 1)
    sum_b(1, 0)
    sum_a(1, 0)
    gw.part_b(1)
    sum_b(0, 2)
    sum_a(0, 2)
    gw.part_a(1)
    sum_b(1, 1)
    sum_a(1, 1)
    gw.part_b(2)
    for c in moments:
        c.wait()
    final_sum(0)
    step_adam(0)
    gn.start()
    sum_b(1, 2)
    sum_a(1, 2)
    gw.part_a(2)
    gn.part_b(0)
    gn.part_a(0)
    final_sum(1)
    step_adam(1)
    gm.start()

    writes = []

    def write(src, dst):
        c = pltpu.make_async_copy(src, dst, out_sem.at[len(writes)])
        c.start()
        writes.append(c)

    write(nm_ref, nm_hbm)
    write(n1_ref, n1_hbm)
    write(n2_ref, n2_hbm)
    gw.part_b(3)
    gn.part_b(1)
    gn.part_a(1)
    gm.part_b(0)
    gw.finish_x()
    gm.part_a(0)
    gn.part_b(2)
    gn.part_a(2)
    gm.part_b(1)
    gm.part_a(1)
    gn.part_b(3)
    gm.part_b(2)
    gm.part_a(2)
    gm.part_b(3)

    wx[k] = w_buf[pl.ds(X * k, X)]
    for j in range(1, T):
        src = (k + T - j) % T
        got(None, lambda: rc(act.at[src], act.at[src], act_s.at[j - 1], act_r.at[j - 1], {"tensor": src}))
        for xx in range(X):
            for part in range(2):
                got(
                    None,
                    lambda: rc(
                        w_part(wx, src, xx, part), w_part(wx, src, xx, part),
                        ws.at[0], wr.at[(src * X + xx) * 2 + part], {"tensor": src},
                    ),
                )

    for i in range(tok // step_t):
        here = pl.ds(i * step_t, step_t)
        for xx in range(X):
            total = None
            for src in range(T):
                part = lax.dot_general(
                    act[src, here, :], wx[src, xx], (((1,), (1,)), ((), ())), preferred_element_type=F32
                )
                total = part if total is None else total + part
            gi_ref[here, xx * rows:(xx + 1) * rows] = total.astype(BF16)
        write(gi_ref.at[here, :], gi_hbm.at[here, :])

    for j in range(Z):
        gn.finish_x(j)
        gm.finish_x(j)
        both = pl.ds(X * ((z + j) % Z), X)
        write(nw_ref.at[both], nw_hbm.at[both])
    for c in writes:
        c.wait()
    for cond, make in pend:
        when(cond, lambda: make().wait_send())


def place(*refs):
    srcs, dsts, held, sems = refs[:5], refs[5:10], refs[10:15], refs[15]
    into, out = [], []
    for src, dst, buf in zip(srcs, dsts, held):
        step = src.shape[0] // PIECES
        for i in range(PIECES):
            here, j = pl.ds(i * step, step), len(into)
            into.append(pltpu.make_async_copy(src.at[here], buf.at[here], sems.at[0, j]))
            out.append(pltpu.make_async_copy(buf.at[here], dst.at[here], sems.at[1, j]))
    for c in into:
        c.start()
    for c, d in zip(into, out):
        c.wait()
        d.start()
    for d in out:
        d.wait()


def local_kernel(inputs, pre_act, grad_hidden, master, moment_one, moment_two):
    tok, hid = pre_act.shape
    rows = master.shape[0]
    n, half = Z * X, rows // 2
    gb = hid - G_SPLIT
    vmem = pl.BlockSpec(memory_space=pltpu.VMEM)
    dma = pltpu.SemaphoreType.DMA
    anywhere, hbm = pl.BlockSpec(memory_space=pl.ANY), pl.BlockSpec(memory_space=pltpu.HBM)
    out = pl.pallas_call(
        kernel,
        out_shape=(
            jax.ShapeDtypeStruct((tok, rows * X), BF16),
            *[jax.ShapeDtypeStruct((rows, hid), F32)] * 3,
            jax.ShapeDtypeStruct((n, rows, hid), BF16),
        ),
        in_specs=[anywhere, vmem, vmem, vmem, anywhere, anywhere],
        out_specs=[anywhere] * 5,
        scratch_shapes=[
            pltpu.VMEM((tok, rows * X), BF16),
            *[pltpu.VMEM((rows, hid), F32)] * 3,
            pltpu.VMEM((n, rows, hid), BF16),
            pltpu.VMEM((rows, hid), F32),
            pltpu.VMEM((rows, hid), F32),
            pltpu.VMEM((n, tok, rows), BF16),
            pltpu.VMEM((n, rows, hid), BF16),
            pltpu.VMEM((T, X, rows, hid), BF16),
            pltpu.VMEM((T, tok, hid), BF16),
            pltpu.VMEM((hid, tok), BF16),
            pltpu.VMEM((2, n, hid, half), BF16),
            pltpu.VMEM((2, Z, G_SPLIT, half), BF16),
            *[pltpu.VMEM((2, Z - 1, G_SPLIT, half), BF16)] * 4,
            *[pltpu.VMEM((2, Z - 1, X, gb, half), BF16)] * 4,
            pltpu.VMEM((2, X, gb, half), F32),
            pltpu.VMEM((2, 2, gb, half), BF16),
            pltpu.VMEM((2, hid, half), F32),
            dma((tok // 256 + Z + 3,)), dma((2,)), dma((n,)), dma((T - 1,)), dma((T - 1,)),
            dma((Z * X * 2,)), dma((T * X * 2,)),
            dma((2, 17)), dma((2, 17)), dma((2, 17)),
            dma((2, Z)), dma((2, Z)),
            dma((2, 6)), dma((2, 6)), dma((2, 6)), dma((2, 6)),
            dma((2,)), dma((2,)),
        ],
        compiler_params=pltpu.CompilerParams(
            collective_id=0, has_side_effects=True, vmem_limit_bytes=60 * 1024 * 1024
        ),
        cost_estimate=pl.CostEstimate(
            flops=4 * tok * rows * n * hid, bytes_accessed=2 * tok * rows * n * 2, transcendentals=tok * hid
        ),
    )(inputs, pre_act, grad_hidden, master, moment_one, moment_two)
    out = pl.pallas_call(
        place,
        out_shape=tuple(jax.ShapeDtypeStruct(a.shape, a.dtype) for a in out),
        in_specs=[hbm] * 5,
        out_specs=[hbm] * 5,
        scratch_shapes=[*[pltpu.VMEM(a.shape, a.dtype) for a in out], dma((2, 5 * PIECES))],
        compiler_params=pltpu.CompilerParams(vmem_limit_bytes=60 * 1024 * 1024),
        cost_estimate=pl.CostEstimate(flops=0, bytes_accessed=2 * 9 * 2**20, transcendentals=0),
    )(*out)
    return (*out[:4], out[4].reshape(n * rows, hid))


def local_plain(inputs, pre_act, grad_hidden, master, moment_one, moment_two):
    act_grad = (grad_hidden.astype(F32) * gelu_slope(pre_act.astype(F32))).astype(BF16)
    weights = lax.all_gather(master.astype(BF16), "dp", axis=0, tiled=True)
    rows = lax.all_to_all(weights, "tensor", split_axis=0, concat_axis=1, tiled=True)
    acts = lax.all_gather(act_grad, "tensor", axis=1, tiled=True)
    grad_input = jnp.einsum("th,dh->td", acts, rows, preferred_element_type=F32).astype(BF16)
    term = jnp.einsum("tr,th->rh", inputs, act_grad, preferred_element_type=F32)
    codes, scale = encode(term)
    grad = lax.psum_scatter(decode(codes, scale), "dp", scatter_dimension=0, tiled=True)
    new_master, new_one, new_two = adam(grad, master, moment_one, moment_two)
    new_weights = lax.all_gather(new_master.astype(BF16), "dp", axis=0, tiled=True)
    return (grad_input, new_master, new_one, new_two, new_weights)


def solution(mesh):
    sizes = dict(mesh.shape)
    body = local_kernel if sizes == {"dp": Z * X, "tensor": T} else local_plain
    two = P("dp", "tensor")
    return jax.shard_map(
        body,
        mesh=mesh,
        in_specs=(P("dp", None), two, two, two, two, two),
        out_specs=(two, two, two, two, P(None, "tensor")),
        check_vma=False,
    )
```

```python
import functools
import math

import jax
import jax.numpy as jnp
from jax import lax
from jax.experimental import pallas as pl
from jax.experimental.pallas import tpu as pltpu
from jax.sharding import PartitionSpec as P

QBLOCK = 256
ADAM_STEP = 10
Z, X, T = 4, 2, 4
W_SPLIT = 464
G_SPLIT = 160
N_SPLIT = 352
PIECES = 4
MESH = pl.DeviceIdType.MESH
F32, BF16 = jnp.float32, jnp.bfloat16


def gelu_slope(value):
    cdf = 0.5 * (1.0 + lax.erf(value * (1.0 / math.sqrt(2.0))))
    pdf = jnp.exp(-0.5 * value * value) / math.sqrt(2.0 * math.pi)
    return cdf + value * pdf


def encode(term):
    rows, cols = term.shape
    blocks = term.reshape(rows, cols // QBLOCK, QBLOCK)
    scale = (jnp.max(jnp.abs(blocks), axis=2) + 1e-06) / 127.0
    codes = jnp.clip(blocks / scale[:, :, None], -127.0, 127.0).astype(BF16)
    return (codes.reshape(rows, cols), scale)


def decode(codes, scale):
    rows, cols = codes.shape
    blocks = codes.astype(F32).reshape(rows, cols // QBLOCK, QBLOCK)
    return (blocks * scale[:, :, None]).reshape(rows, cols)


def adam(grad, master, moment_one, moment_two):
    new_one = 0.9 * moment_one + 0.1 * grad
    new_two = 0.999 * moment_two + 0.001 * grad * grad
    corr_one = 1.0 - 0.9**ADAM_STEP
    corr_two = 1.0 - 0.999**ADAM_STEP
    update = new_one / corr_one / (jnp.sqrt(new_two / corr_two) + 1e-08) + 0.01 * master
    return master - 0.01 * update, new_one, new_two


def kernel(
    in_hbm, pre_ref, hid_ref, master_ref, one_hbm, two_hbm,
    gi_hbm, nm_hbm, n1_hbm, n2_hbm, nw_hbm,
    gi_ref, nm_ref, n1_ref, n2_ref, nw_ref, one_ref, two_ref,
    xin, w_buf, wx, act, act_t, term, xr, zua, zda, sua, sda, zub, zdb, sub, sdb, fxs, fxr, grad_t,
    out_sem, mom_sem, in_sem, act_s, act_r, ws, wr, wag, nag, mag, rxs, rxr, ras, rar, rbs, rbr, fs, fr,
):
    r = lax.axis_index("dp")
    k = lax.axis_index("tensor")
    z, x = r // X, r % X
    o = 1 - x
    across, above, below = {"dp": r + 1 - 2 * x}, {"dp": r + X}, {"dp": r - X}
    up_ok, dn_ok = z <= Z - 2, z >= 1
    tok, hid = pre_ref.shape
    rows = master_ref.shape[0]
    pend = []

    def when(cond, fn):
        if cond is None:
            fn()
        else:
            pl.when(cond)(fn)

    def rc(src, dst, ssem, rsem, dev):
        return pltpu.make_async_remote_copy(
            src_ref=src, dst_ref=dst, send_sem=ssem, recv_sem=rsem, device_id=dev, device_id_type=MESH
        )

    def send(cond, make):
        when(cond, lambda: make().start())
        pend.append((cond, make))

    def got(cond, make):
        when(cond, lambda: make().wait_recv())

    class Gather:
        def __init__(self, buf, sems, first, split, end, on_block, late):
            self.buf, self.s, self.on = buf, sems, on_block
            self.rows_a, self.rows_b = pl.ds(first, split - first), pl.ds(split, end - split)
            self.late, self.kept = late, []

        def a(self, zz, xx):
            return self.buf.at[X * zz + xx, self.rows_a, :]

        def b(self, zz):
            return self.buf.at[pl.ds(X * zz, X), self.rows_b, :]

        def b1(self, zz, xx):
            return self.buf.at[X * zz + xx, self.rows_b, :]

        def mk(self, ref, idx, dev):
            return lambda: rc(ref(), ref(), self.s.at[0, idx], self.s.at[1, idx], dev)

        def za(self, s):
            zz_u, zz_d = z - s, z + s
            send(up_ok & (zz_u >= 0), self.mk(lambda: self.a(zz_u, x), s, above))
            send(dn_ok & (zz_d <= Z - 1), self.mk(lambda: self.a(zz_d, x), 3 + s, below))

        def zb(self, s):
            zz_u, zz_d = z - s, z + s
            send(up_ok & (zz_u >= 0), self.mk(lambda: self.b(zz_u), 6 + s, above))
            send(dn_ok & (zz_d <= Z - 1), self.mk(lambda: self.b(zz_d), 9 + s, below))

        def xa(self, cond, zz):
            if self.late:
                self.kept.append((cond, zz))
            else:
                self.xa_now(cond, zz)

        def flush(self):
            for cond, zz in self.kept:
                self.xa_now(cond, zz)
            self.kept = []

        def xa_now(self, cond, zz):
            send(cond, self.mk(lambda: self.a(zz, x), 12 + zz, across))

        def start(self):
            self.xa(None, z)
            self.za(0)
            send(None, self.mk(lambda: self.b1(z, x), 16, across))
            self.on(None, z, x, 0)

        def part_a(self, s):
            zu, zd = z - 1 - s, z + 1 + s
            cu, cd = zu >= 0, zd <= Z - 1
            got(cu, self.mk(lambda: self.a(zu, x), s, above))
            got(cd, self.mk(lambda: self.a(zd, x), 3 + s, below))
            if s + 1 < Z - 1:
                self.za(s + 1)
            self.xa(cu, zu)
            self.xa(cd, zd)
            self.on(cu, zu, x, 0)
            self.on(cd, zd, x, 0)

        def part_b(self, s):
            if s == 0:
                got(None, self.mk(lambda: self.b1(z, o), 16, across))
            else:
                zu, zd = z - s, z + s
                cu, cd = zu >= 0, zd <= Z - 1
                got(cu, self.mk(lambda: self.b(zu), 6 + s - 1, above))
                got(cd, self.mk(lambda: self.b(zd), 9 + s - 1, below))
            if s < Z - 1:
                self.zb(s)
            if s == 0:
                for xx in range(X):
                    self.on(None, z, xx, 1)
            else:
                for xx in range(X):
                    self.on(cu, zu, xx, 1)
                    self.on(cd, zd, xx, 1)

        def finish_x(self, *only):
            for j in only or range(Z):
                zz = (z + j) % Z
                got(None, self.mk(lambda: self.a(zz, o), 12 + zz, across))
                self.on(None, zz, o, 0)

    def w_part(ref, idx, xx, part):
        lo, n = (0, W_SPLIT) if part == 0 else (W_SPLIT, rows - W_SPLIT)
        return ref.at[idx, xx, pl.ds(lo, n), :]

    def to_tensor(cond, zz, xx, part):
        lo, n = (0, W_SPLIT) if part == 0 else (W_SPLIT, rows - W_SPLIT)
        sem = (zz * X + xx) * 2 + part
        rsem = (k * X + xx) * 2 + part
        c = zz != k
        send(
            c if cond is None else cond & c,
            lambda: rc(
                w_buf.at[X * zz + xx, pl.ds(lo, n), :], w_part(wx, k, xx, part),
                ws.at[sem], wr.at[rsem], {"tensor": zz},
            ),
        )

    half = rows // 2
    gw = Gather(w_buf, wag, 0, W_SPLIT, rows, to_tensor, False)
    gn, gm = [
        Gather(nw_ref, sems, i * half, i * half + N_SPLIT, (i + 1) * half, lambda *_: None, False)
        for i, sems in enumerate((nag, mag))
    ]

    hi = z // 2
    order = [3 - 3 * hi, 2 - hi, 1 - z + 4 * hi, z]

    def fetch(j):
        blk = X * order[j // 2] + (o if j % 2 == 0 else x)
        col = pl.multiple_of(blk * rows, 128)
        return pltpu.make_async_copy(in_hbm.at[:, pl.ds(col, rows)], xin.at[j], in_sem.at[j])

    for j in range(Z * X):
        fetch(j).start()
    moments = [
        pltpu.make_async_copy(one_hbm, one_ref, mom_sem.at[0]),
        pltpu.make_async_copy(two_hbm, two_ref, mom_sem.at[1]),
    ]
    for c in moments:
        c.start()
    w_buf[r] = master_ref[...].astype(BF16)

    barrier = pltpu.get_barrier_semaphore()

    def hello(dev):
        pl.semaphore_signal(barrier, inc=1, device_id=dev, device_id_type=MESH)

    hello(across)
    when(up_ok, lambda: hello(above))
    when(dn_ok, lambda: hello(below))
    for j in range(1, T):
        hello({"tensor": (k + j) % T})
    pl.semaphore_wait(barrier, T + 1 + z * (Z - 1 - z) // 2)

    gw.start()

    step_t = 256

    @pl.loop(0, tok // step_t)
    def _(i):
        here = pl.ds(pl.multiple_of(i * step_t, step_t), step_t)
        val = hid_ref[here, :].astype(F32) * gelu_slope(pre_ref[here, :].astype(F32))
        act[k, here, :] = val.astype(BF16)
        act_t[:, here] = val.T.astype(BF16)

    def make_term(h, j):
        blk = X * order[j // 2] + (o if j % 2 == 0 else x)
        if h == 0:
            fetch(j).wait()

        t = jnp.dot(act_t[...], xin[j, :, pl.ds(h * half, half)], preferred_element_type=F32)
        scale = (jnp.max(jnp.abs(t), axis=0, keepdims=True) + 1e-06) / 127.0
        codes = jnp.clip(t * (1.0 / scale), -127.0, 127.0).astype(BF16)
        term[h, blk] = (codes.astype(F32) * scale).astype(BF16)

    def xr_copy(h, t, own):
        return lambda: rc(
            term.at[h, X * t + own, pl.ds(0, G_SPLIT), :], xr.at[h, t], rxs.at[h, t], rxr.at[h, t], across
        )

    def z_sum(s, value, arrived, zu, zd, su, sd, ssem, rsem):
        tu, td = z + 3 - s, z - 3 + s
        cu, cd = up_ok & (z <= s), dn_ok & (z >= 3 - s)
        for cond, edge, t, zin, out, base, dev in (
            (cu, z == 0, tu, zu, su, 0, above),
            (cd, z == Z - 1, td, zd, sd, 3, below),
        ):
            make = lambda zin=zin, out=out, base=base, dev=dev: rc(
                out.at[s], zin.at[s], ssem.at[base + s], rsem.at[base + s], dev
            )
            def body(edge=edge, t=t, zin=zin, out=out, base=base, dev=dev, make=make):
                arrived(t)
                own = value(t)

                @pl.when(edge)
                def _():
                    out[s] = own().astype(BF16)

                if s > 0:
                    @pl.when(jnp.logical_not(edge))
                    def _():
                        rc(out.at[s], zin.at[s - 1], ssem.at[base + s - 1], rsem.at[base + s - 1], dev).wait_recv()
                        out[s] = (own() + zin[s - 1].astype(F32)).astype(BF16)

            pl.when(cond)(body)
            send(cond, make)

    def value_a(h, t):
        return lambda: term[h, X * t + x, :G_SPLIT, :].astype(F32) + xr[h, t].astype(F32)

    def value_b(h, t):
        return lambda: term[h, pl.ds(X * t, X), G_SPLIT:, :].astype(F32)

    def arrived_a(h, t):
        xr_copy(h, t, o)().wait_recv()

    def sum_a(h, s):
        z_sum(
            s, lambda t: value_a(h, t), lambda t: arrived_a(h, t),
            zua.at[h], zda.at[h], sua.at[h], sda.at[h], ras.at[h], rar.at[h],
        )

    def sum_b(h, s):
        z_sum(
            s, lambda t: value_b(h, t), lambda t: None,
            zub.at[h], zdb.at[h], sub.at[h], sdb.at[h], rbs.at[h], rbr.at[h],
        )

    last = Z - 2

    def final_sum(h):
        sb, ga = fxs.at[h], grad_t.at[h, pl.ds(0, G_SPLIT), :]
        sb[...] = value_b(h, z)()
        for cond, zin, base, dev in ((dn_ok, zub, 0, above), (up_ok, zdb, 3, below)):
            def body(zin=zin, base=base, dev=dev):
                slot = zin.at[h, last]
                rc(slot, slot, rbs.at[h, base + last], rbr.at[h, base + last], dev).wait_recv()
                sb[...] += slot[...].astype(F32)
            pl.when(cond)(body)
        fxr[h, 0] = sb[o].astype(BF16)
        fx = lambda: rc(fxr.at[h, 0], fxr.at[h, 1], fs.at[h], fr.at[h], across)
        send(None, fx)
        arrived_a(h, z)
        ga[...] = value_a(h, z)()
        for cond, zin, base, dev in ((dn_ok, zua, 0, above), (up_ok, zda, 3, below)):
            def body(zin=zin, base=base, dev=dev):
                slot = zin.at[h, last]
                rc(slot, slot, ras.at[h, base + last], rar.at[h, base + last], dev).wait_recv()
                ga[...] += slot[...].astype(F32)
            pl.when(cond)(body)
        fx().wait_recv()
        grad_t[h, G_SPLIT:, :] = sb[x] + fxr[h, 1].astype(F32)

    def step_adam(h):
        @pl.loop(0, half // 128)
        def _(c):
            at = pl.multiple_of(c * 128, 128)
            here = pl.ds(h * half + at, 128)
            nm, n1, n2 = adam(
                grad_t[h, :, pl.ds(at, 128)].T, master_ref[here, :], one_ref[here, :], two_ref[here, :]
            )
            nm_ref[here, :] = nm
            n1_ref[here, :] = n1
            n2_ref[here, :] = n2
            nw_ref[r, here, :] = nm.astype(BF16)

    def terms(h, i):
        make_term(h, 2 * i)
        send(None, xr_copy(h, order[i], o))
        make_term(h, 2 * i + 1)

    terms(0, 0)
    gw.part_b(0)
    terms(0, 1)
    terms(0, 2)
    gw.part_a(0)
    terms(0, 3)
    sum_b(0, 0)
    sum_a(0, 0)
    for j in range(1, T):
        kk = (k + j) % T
        send(
            None,
            lambda kk=kk, j=j: rc(act.at[k], act.at[k], act_s.at[j - 1], act_r.at[j - 1], {"tensor": kk}),
        )
    terms(1, 0)
    terms(1, 1)
    sum_b(0, 1)
    gw.part_b(1)
    terms(1, 2)
    sum_a(0, 1)
    terms(1, 3)
    sum_b(1, 0)
    sum_a(1, 0)
    sum_b(0, 2)
    sum_a(0, 2)
    gw.part_a(1)
    sum_b(1, 1)
    sum_a(1, 1)
    gw.part_b(2)
    for c in moments:
        c.wait()
    final_sum(0)
    step_adam(0)
    gn.start()
    sum_b(1, 2)
    sum_a(1, 2)
    gw.part_a(2)
    gn.part_b(0)
    gn.part_a(0)
    final_sum(1)
    step_adam(1)
    gm.start()

    writes = []

    def write(src, dst):
        c = pltpu.make_async_copy(src, dst, out_sem.at[len(writes)])
        c.start()
        writes.append(c)

    write(nm_ref, nm_hbm)
    write(n1_ref, n1_hbm)
    write(n2_ref, n2_hbm)
    gw.part_b(3)
    gn.part_b(1)
    gn.part_a(1)
    gm.part_b(0)
    gw.finish_x()
    gm.part_a(0)
    gn.part_b(2)
    gn.part_a(2)
    gm.part_b(1)
    gm.part_a(1)
    gn.part_b(3)
    gm.part_b(2)
    gm.part_a(2)
    gm.part_b(3)

    wx[k] = w_buf[pl.ds(X * k, X)]
    for j in range(1, T):
        src = (k + T - j) % T
        got(None, lambda: rc(act.at[src], act.at[src], act_s.at[j - 1], act_r.at[j - 1], {"tensor": src}))
        for xx in range(X):
            for part in range(2):
                got(
                    None,
                    lambda: rc(
                        w_part(wx, src, xx, part), w_part(wx, src, xx, part),
                        ws.at[0], wr.at[(src * X + xx) * 2 + part], {"tensor": src},
                    ),
                )

    for i in range(tok // step_t):
        here = pl.ds(i * step_t, step_t)
        for xx in range(X):
            total = None
            for src in range(T):
                part = lax.dot_general(
                    act[src, here, :], wx[src, xx], (((1,), (1,)), ((), ())), preferred_element_type=F32
                )
                total = part if total is None else total + part
            gi_ref[here, xx * rows:(xx + 1) * rows] = total.astype(BF16)
        write(gi_ref.at[here, :], gi_hbm.at[here, :])

    for j in range(Z):
        gn.finish_x(j)
        gm.finish_x(j)
        both = pl.ds(X * ((z + j) % Z), X)
        write(nw_ref.at[both], nw_hbm.at[both])
    for c in writes:
        c.wait()
    for cond, make in pend:
        when(cond, lambda: make().wait_send())


def place(*refs):
    srcs, dsts, held, sems = refs[:5], refs[5:10], refs[10:15], refs[15]
    into, out = [], []
    for src, dst, buf in zip(srcs, dsts, held):
        step = src.shape[0] // PIECES
        for i in range(PIECES):
            here, j = pl.ds(i * step, step), len(into)
            into.append(pltpu.make_async_copy(src.at[here], buf.at[here], sems.at[0, j]))
            out.append(pltpu.make_async_copy(buf.at[here], dst.at[here], sems.at[1, j]))
    for c in into:
        c.start()
    for c, d in zip(into, out):
        c.wait()
        d.start()
    for d in out:
        d.wait()


def local_kernel(inputs, pre_act, grad_hidden, master, moment_one, moment_two):
    tok, hid = pre_act.shape
    rows = master.shape[0]
    n, half = Z * X, rows // 2
    gb = hid - G_SPLIT
    vmem = pl.BlockSpec(memory_space=pltpu.VMEM)
    dma = pltpu.SemaphoreType.DMA
    anywhere, hbm = pl.BlockSpec(memory_space=pl.ANY), pl.BlockSpec(memory_space=pltpu.HBM)
    out = pl.pallas_call(
        kernel,
        out_shape=(
            jax.ShapeDtypeStruct((tok, rows * X), BF16),
            *[jax.ShapeDtypeStruct((rows, hid), F32)] * 3,
            jax.ShapeDtypeStruct((n, rows, hid), BF16),
        ),
        in_specs=[anywhere, vmem, vmem, vmem, anywhere, anywhere],
        out_specs=[anywhere] * 5,
        scratch_shapes=[
            pltpu.VMEM((tok, rows * X), BF16),
            *[pltpu.VMEM((rows, hid), F32)] * 3,
            pltpu.VMEM((n, rows, hid), BF16),
            pltpu.VMEM((rows, hid), F32),
            pltpu.VMEM((rows, hid), F32),
            pltpu.VMEM((n, tok, rows), BF16),
            pltpu.VMEM((n, rows, hid), BF16),
            pltpu.VMEM((T, X, rows, hid), BF16),
            pltpu.VMEM((T, tok, hid), BF16),
            pltpu.VMEM((hid, tok), BF16),
            pltpu.VMEM((2, n, hid, half), BF16),
            pltpu.VMEM((2, Z, G_SPLIT, half), BF16),
            *[pltpu.VMEM((2, Z - 1, G_SPLIT, half), BF16)] * 4,
            *[pltpu.VMEM((2, Z - 1, X, gb, half), BF16)] * 4,
            pltpu.VMEM((2, X, gb, half), F32),
            pltpu.VMEM((2, 2, gb, half), BF16),
            pltpu.VMEM((2, hid, half), F32),
            dma((tok // 256 + Z + 3,)), dma((2,)), dma((n,)), dma((T - 1,)), dma((T - 1,)),
            dma((Z * X * 2,)), dma((T * X * 2,)),
            dma((2, 17)), dma((2, 17)), dma((2, 17)),
            dma((2, Z)), dma((2, Z)),
            dma((2, 6)), dma((2, 6)), dma((2, 6)), dma((2, 6)),
            dma((2,)), dma((2,)),
        ],
        compiler_params=pltpu.CompilerParams(
            collective_id=0, has_side_effects=True, vmem_limit_bytes=60 * 1024 * 1024
        ),
        cost_estimate=pl.CostEstimate(
            flops=4 * tok * rows * n * hid, bytes_accessed=2 * tok * rows * n * 2, transcendentals=tok * hid
        ),
    )(inputs, pre_act, grad_hidden, master, moment_one, moment_two)
    out = pl.pallas_call(
        place,
        out_shape=tuple(jax.ShapeDtypeStruct(a.shape, a.dtype) for a in out),
        in_specs=[hbm] * 5,
        out_specs=[hbm] * 5,
        scratch_shapes=[*[pltpu.VMEM(a.shape, a.dtype) for a in out], dma((2, 5 * PIECES))],
        compiler_params=pltpu.CompilerParams(vmem_limit_bytes=60 * 1024 * 1024),
        cost_estimate=pl.CostEstimate(flops=0, bytes_accessed=2 * 9 * 2**20, transcendentals=0),
    )(*out)
    return (*out[:4], out[4].reshape(n * rows, hid))


def local_plain(inputs, pre_act, grad_hidden, master, moment_one, moment_two):
    act_grad = (grad_hidden.astype(F32) * gelu_slope(pre_act.astype(F32))).astype(BF16)
    weights = lax.all_gather(master.astype(BF16), "dp", axis=0, tiled=True)
    rows = lax.all_to_all(weights, "tensor", split_axis=0, concat_axis=1, tiled=True)
    acts = lax.all_gather(act_grad, "tensor", axis=1, tiled=True)
    grad_input = jnp.einsum("th,dh->td", acts, rows, preferred_element_type=F32).astype(BF16)
    term = jnp.einsum("tr,th->rh", inputs, act_grad, preferred_element_type=F32)
    codes, scale = encode(term)
    grad = lax.psum_scatter(decode(codes, scale), "dp", scatter_dimension=0, tiled=True)
    new_master, new_one, new_two = adam(grad, master, moment_one, moment_two)
    new_weights = lax.all_gather(new_master.astype(BF16), "dp", axis=0, tiled=True)
    return (grad_input, new_master, new_one, new_two, new_weights)


def solution(mesh):
    sizes = dict(mesh.shape)
    body = local_kernel if sizes == {"dp": Z * X, "tensor": T} else local_plain
    two = P("dp", "tensor")
    return jax.shard_map(
        body,
        mesh=mesh,
        in_specs=(P("dp", None), two, two, two, two, two),
        out_specs=(two, two, two, two, P(None, "tensor")),
        check_vma=False,
    )
```

```python
import functools
import math

import jax
import jax.numpy as jnp
from jax import lax
from jax.experimental import pallas as pl
from jax.experimental.pallas import tpu as pltpu
from jax.sharding import PartitionSpec as P

QBLOCK = 256
ADAM_STEP = 10
Z, X, T = 4, 2, 4
W_SPLIT = 544
G_SPLIT = 160
N_SPLIT = 352
PIECES = 4
MESH = pl.DeviceIdType.MESH
F32, BF16 = jnp.float32, jnp.bfloat16


def gelu_slope(value):
    cdf = 0.5 * (1.0 + lax.erf(value * (1.0 / math.sqrt(2.0))))
    pdf = jnp.exp(-0.5 * value * value) / math.sqrt(2.0 * math.pi)
    return cdf + value * pdf


def encode(term):
    rows, cols = term.shape
    blocks = term.reshape(rows, cols // QBLOCK, QBLOCK)
    scale = (jnp.max(jnp.abs(blocks), axis=2) + 1e-06) / 127.0
    codes = jnp.clip(blocks / scale[:, :, None], -127.0, 127.0).astype(BF16)
    return (codes.reshape(rows, cols), scale)


def decode(codes, scale):
    rows, cols = codes.shape
    blocks = codes.astype(F32).reshape(rows, cols // QBLOCK, QBLOCK)
    return (blocks * scale[:, :, None]).reshape(rows, cols)


def adam(grad, master, moment_one, moment_two):
    new_one = 0.9 * moment_one + 0.1 * grad
    new_two = 0.999 * moment_two + 0.001 * grad * grad
    corr_one = 1.0 - 0.9**ADAM_STEP
    corr_two = 1.0 - 0.999**ADAM_STEP
    update = new_one / corr_one / (jnp.sqrt(new_two / corr_two) + 1e-08) + 0.01 * master
    return master - 0.01 * update, new_one, new_two


def kernel(
    in_hbm, pre_ref, hid_ref, master_ref, one_hbm, two_hbm,
    gi_hbm, nm_hbm, n1_hbm, n2_hbm, nw_hbm,
    gi_ref, nm_ref, n1_ref, n2_ref, nw_ref, one_ref, two_ref,
    xin, w_buf, wx, act, act_t, term, xr, zua, zda, sua, sda, zub, zdb, sub, sdb, fxs, fxr, grad_t,
    out_sem, mom_sem, in_sem, act_s, act_r, ws, wr, wag, nag, mag, rxs, rxr, ras, rar, rbs, rbr, fs, fr,
):
    r = lax.axis_index("dp")
    k = lax.axis_index("tensor")
    z, x = r // X, r % X
    o = 1 - x
    across, above, below = {"dp": r + 1 - 2 * x}, {"dp": r + X}, {"dp": r - X}
    up_ok, dn_ok = z <= Z - 2, z >= 1
    tok, hid = pre_ref.shape
    rows = master_ref.shape[0]
    pend = []

    def when(cond, fn):
        if cond is None:
            fn()
        else:
            pl.when(cond)(fn)

    def rc(src, dst, ssem, rsem, dev):
        return pltpu.make_async_remote_copy(
            src_ref=src, dst_ref=dst, send_sem=ssem, recv_sem=rsem, device_id=dev, device_id_type=MESH
        )

    def send(cond, make):
        when(cond, lambda: make().start())
        pend.append((cond, make))

    def got(cond, make):
        when(cond, lambda: make().wait_recv())

    class Gather:
        def __init__(self, buf, sems, first, split, end, on_block, late):
            self.buf, self.s, self.on = buf, sems, on_block
            self.rows_a, self.rows_b = pl.ds(first, split - first), pl.ds(split, end - split)
            self.late, self.kept = late, []

        def a(self, zz, xx):
            return self.buf.at[X * zz + xx, self.rows_a, :]

        def b(self, zz):
            return self.buf.at[pl.ds(X * zz, X), self.rows_b, :]

        def b1(self, zz, xx):
            return self.buf.at[X * zz + xx, self.rows_b, :]

        def mk(self, ref, idx, dev):
            return lambda: rc(ref(), ref(), self.s.at[0, idx], self.s.at[1, idx], dev)

        def za(self, s):
            zz_u, zz_d = z - s, z + s
            send(up_ok & (zz_u >= 0), self.mk(lambda: self.a(zz_u, x), s, above))
            send(dn_ok & (zz_d <= Z - 1), self.mk(lambda: self.a(zz_d, x), 3 + s, below))

        def zb(self, s):
            zz_u, zz_d = z - s, z + s
            send(up_ok & (zz_u >= 0), self.mk(lambda: self.b(zz_u), 6 + s, above))
            send(dn_ok & (zz_d <= Z - 1), self.mk(lambda: self.b(zz_d), 9 + s, below))

        def xa(self, cond, zz):
            if self.late:
                self.kept.append((cond, zz))
            else:
                self.xa_now(cond, zz)

        def flush(self):
            for cond, zz in self.kept:
                self.xa_now(cond, zz)
            self.kept = []

        def xa_now(self, cond, zz):
            send(cond, self.mk(lambda: self.a(zz, x), 12 + zz, across))

        def start(self):
            self.xa(None, z)
            self.za(0)
            send(None, self.mk(lambda: self.b1(z, x), 16, across))
            self.on(None, z, x, 0)

        def part_a(self, s):
            zu, zd = z - 1 - s, z + 1 + s
            cu, cd = zu >= 0, zd <= Z - 1
            got(cu, self.mk(lambda: self.a(zu, x), s, above))
            got(cd, self.mk(lambda: self.a(zd, x), 3 + s, below))
            if s + 1 < Z - 1:
                self.za(s + 1)
            self.xa(cu, zu)
            self.xa(cd, zd)
            self.on(cu, zu, x, 0)
            self.on(cd, zd, x, 0)

        def part_b(self, s):
            if s == 0:
                got(None, self.mk(lambda: self.b1(z, o), 16, across))
            else:
                zu, zd = z - s, z + s
                cu, cd = zu >= 0, zd <= Z - 1
                got(cu, self.mk(lambda: self.b(zu), 6 + s - 1, above))
                got(cd, self.mk(lambda: self.b(zd), 9 + s - 1, below))
            if s < Z - 1:
                self.zb(s)
            if s == 0:
                for xx in range(X):
                    self.on(None, z, xx, 1)
            else:
                for xx in range(X):
                    self.on(cu, zu, xx, 1)
                    self.on(cd, zd, xx, 1)

        def finish_x(self, *only):
            for j in only or range(Z):
                zz = (z + j) % Z
                got(None, self.mk(lambda: self.a(zz, o), 12 + zz, across))
                self.on(None, zz, o, 0)

    def w_part(ref, idx, xx, part):
        lo, n = (0, W_SPLIT) if part == 0 else (W_SPLIT, rows - W_SPLIT)
        return ref.at[idx, xx, pl.ds(lo, n), :]

    def to_tensor(cond, zz, xx, part):
        lo, n = (0, W_SPLIT) if part == 0 else (W_SPLIT, rows - W_SPLIT)
        sem = (zz * X + xx) * 2 + part
        rsem = (k * X + xx) * 2 + part
        c = zz != k
        send(
            c if cond is None else cond & c,
            lambda: rc(
                w_buf.at[X * zz + xx, pl.ds(lo, n), :], w_part(wx, k, xx, part),
                ws.at[sem], wr.at[rsem], {"tensor": zz},
            ),
        )

    half = rows // 2
    gw = Gather(w_buf, wag, 0, W_SPLIT, rows, to_tensor, False)
    gn, gm = [
        Gather(nw_ref, sems, i * half, i * half + N_SPLIT, (i + 1) * half, lambda *_: None, False)
        for i, sems in enumerate((nag, mag))
    ]

    hi = z // 2
    order = [3 - 3 * hi, 2 - hi, 1 - z + 4 * hi, z]

    def fetch(j):
        blk = X * order[j // 2] + (o if j % 2 == 0 else x)
        col = pl.multiple_of(blk * rows, 128)
        return pltpu.make_async_copy(in_hbm.at[:, pl.ds(col, rows)], xin.at[j], in_sem.at[j])

    for j in range(Z * X):
        fetch(j).start()
    moments = [
        pltpu.make_async_copy(one_hbm, one_ref, mom_sem.at[0]),
        pltpu.make_async_copy(two_hbm, two_ref, mom_sem.at[1]),
    ]
    for c in moments:
        c.start()
    w_buf[r] = master_ref[...].astype(BF16)

    barrier = pltpu.get_barrier_semaphore()

    def hello(dev):
        pl.semaphore_signal(barrier, inc=1, device_id=dev, device_id_type=MESH)

    hello(across)
    when(up_ok, lambda: hello(above))
    when(dn_ok, lambda: hello(below))
    for j in range(1, T):
        hello({"tensor": (k + j) % T})
    pl.semaphore_wait(barrier, T + 1 + z * (Z - 1 - z) // 2)

    gw.start()

    step_t = 256

    @pl.loop(0, tok // step_t)
    def _(i):
        here = pl.ds(pl.multiple_of(i * step_t, step_t), step_t)
        val = hid_ref[here, :].astype(F32) * gelu_slope(pre_ref[here, :].astype(F32))
        act[k, here, :] = val.astype(BF16)
        act_t[:, here] = val.T.astype(BF16)

    def make_term(h, j):
        blk = X * order[j // 2] + (o if j % 2 == 0 else x)
        if h == 0:
            fetch(j).wait()

        t = jnp.dot(act_t[...], xin[j, :, pl.ds(h * half, half)], preferred_element_type=F32)
        scale = (jnp.max(jnp.abs(t), axis=0, keepdims=True) + 1e-06) / 127.0
        codes = jnp.clip(t * (1.0 / scale), -127.0, 127.0).astype(BF16)
        term[h, blk] = (codes.astype(F32) * scale).astype(BF16)

    def xr_copy(h, t, own):
        return lambda: rc(
            term.at[h, X * t + own, pl.ds(0, G_SPLIT), :], xr.at[h, t], rxs.at[h, t], rxr.at[h, t], across
        )

    def z_sum(s, value, arrived, zu, zd, su, sd, ssem, rsem):
        tu, td = z + 3 - s, z - 3 + s
        cu, cd = up_ok & (z <= s), dn_ok & (z >= 3 - s)
        for cond, edge, t, zin, out, base, dev in (
            (cu, z == 0, tu, zu, su, 0, above),
            (cd, z == Z - 1, td, zd, sd, 3, below),
        ):
            make = lambda zin=zin, out=out, base=base, dev=dev: rc(
                out.at[s], zin.at[s], ssem.at[base + s], rsem.at[base + s], dev
            )
            def body(edge=edge, t=t, zin=zin, out=out, base=base, dev=dev, make=make):
                arrived(t)
                own = value(t)

                @pl.when(edge)
                def _():
                    out[s] = own().astype(BF16)

                if s > 0:
                    @pl.when(jnp.logical_not(edge))
                    def _():
                        rc(out.at[s], zin.at[s - 1], ssem.at[base + s - 1], rsem.at[base + s - 1], dev).wait_recv()
                        out[s] = (own() + zin[s - 1].astype(F32)).astype(BF16)

            pl.when(cond)(body)
            send(cond, make)

    def value_a(h, t):
        return lambda: term[h, X * t + x, :G_SPLIT, :].astype(F32) + xr[h, t].astype(F32)

    def value_b(h, t):
        return lambda: term[h, pl.ds(X * t, X), G_SPLIT:, :].astype(F32)

    def arrived_a(h, t):
        xr_copy(h, t, o)().wait_recv()

    def sum_a(h, s):
        z_sum(
            s, lambda t: value_a(h, t), lambda t: arrived_a(h, t),
            zua.at[h], zda.at[h], sua.at[h], sda.at[h], ras.at[h], rar.at[h],
        )

    def sum_b(h, s):
        z_sum(
            s, lambda t: value_b(h, t), lambda t: None,
            zub.at[h], zdb.at[h], sub.at[h], sdb.at[h], rbs.at[h], rbr.at[h],
        )

    last = Z - 2

    def final_sum(h):
        sb, ga = fxs.at[h], grad_t.at[h, pl.ds(0, G_SPLIT), :]
        sb[...] = value_b(h, z)()
        for cond, zin, base, dev in ((dn_ok, zub, 0, above), (up_ok, zdb, 3, below)):
            def body(zin=zin, base=base, dev=dev):
                slot = zin.at[h, last]
                rc(slot, slot, rbs.at[h, base + last], rbr.at[h, base + last], dev).wait_recv()
                sb[...] += slot[...].astype(F32)
            pl.when(cond)(body)
        fxr[h, 0] = sb[o].astype(BF16)
        fx = lambda: rc(fxr.at[h, 0], fxr.at[h, 1], fs.at[h], fr.at[h], across)
        send(None, fx)
        arrived_a(h, z)
        ga[...] = value_a(h, z)()
        for cond, zin, base, dev in ((dn_ok, zua, 0, above), (up_ok, zda, 3, below)):
            def body(zin=zin, base=base, dev=dev):
                slot = zin.at[h, last]
                rc(slot, slot, ras.at[h, base + last], rar.at[h, base + last], dev).wait_recv()
                ga[...] += slot[...].astype(F32)
            pl.when(cond)(body)
        fx().wait_recv()
        grad_t[h, G_SPLIT:, :] = sb[x] + fxr[h, 1].astype(F32)

    def step_adam(h):
        @pl.loop(0, half // 128)
        def _(c):
            at = pl.multiple_of(c * 128, 128)
            here = pl.ds(h * half + at, 128)
            nm, n1, n2 = adam(
                grad_t[h, :, pl.ds(at, 128)].T, master_ref[here, :], one_ref[here, :], two_ref[here, :]
            )
            nm_ref[here, :] = nm
            n1_ref[here, :] = n1
            n2_ref[here, :] = n2
            nw_ref[r, here, :] = nm.astype(BF16)

    def terms(h, i):
        make_term(h, 2 * i)
        send(None, xr_copy(h, order[i], o))
        make_term(h, 2 * i + 1)

    terms(0, 0)
    gw.part_b(0)
    terms(0, 1)
    terms(0, 2)
    gw.part_a(0)
    terms(0, 3)
    sum_b(0, 0)
    sum_a(0, 0)
    for j in range(1, T):
        kk = (k + j) % T
        send(
            None,
            lambda kk=kk, j=j: rc(act.at[k], act.at[k], act_s.at[j - 1], act_r.at[j - 1], {"tensor": kk}),
        )
    terms(1, 0)
    terms(1, 1)
    sum_b(0, 1)
    gw.part_b(1)
    terms(1, 2)
    sum_a(0, 1)
    terms(1, 3)
    sum_b(1, 0)
    sum_a(1, 0)
    sum_b(0, 2)
    sum_a(0, 2)
    gw.part_a(1)
    sum_b(1, 1)
    sum_a(1, 1)
    gw.part_b(2)
    for c in moments:
        c.wait()
    final_sum(0)
    step_adam(0)
    gn.start()
    sum_b(1, 2)
    sum_a(1, 2)
    gw.part_a(2)
    gn.part_b(0)
    gn.part_a(0)
    final_sum(1)
    step_adam(1)
    gm.start()

    writes = []

    def write(src, dst):
        c = pltpu.make_async_copy(src, dst, out_sem.at[len(writes)])
        c.start()
        writes.append(c)

    write(nm_ref, nm_hbm)
    write(n1_ref, n1_hbm)
    write(n2_ref, n2_hbm)
    gw.part_b(3)
    gn.part_b(1)
    gn.part_a(1)
    gm.part_b(0)
    gw.finish_x()
    gm.part_a(0)
    gn.part_b(2)
    gn.part_a(2)
    gm.part_b(1)
    gm.part_a(1)
    gn.part_b(3)
    gm.part_b(2)
    gm.part_a(2)
    gm.part_b(3)

    wx[k] = w_buf[pl.ds(X * k, X)]
    for j in range(1, T):
        src = (k + T - j) % T
        got(None, lambda: rc(act.at[src], act.at[src], act_s.at[j - 1], act_r.at[j - 1], {"tensor": src}))
        for xx in range(X):
            for part in range(2):
                got(
                    None,
                    lambda: rc(
                        w_part(wx, src, xx, part), w_part(wx, src, xx, part),
                        ws.at[0], wr.at[(src * X + xx) * 2 + part], {"tensor": src},
                    ),
                )

    for i in range(tok // step_t):
        here = pl.ds(i * step_t, step_t)
        for xx in range(X):
            total = None
            for src in range(T):
                part = lax.dot_general(
                    act[src, here, :], wx[src, xx], (((1,), (1,)), ((), ())), preferred_element_type=F32
                )
                total = part if total is None else total + part
            gi_ref[here, xx * rows:(xx + 1) * rows] = total.astype(BF16)
        write(gi_ref.at[here, :], gi_hbm.at[here, :])

    for j in range(Z):
        gn.finish_x(j)
        gm.finish_x(j)
        both = pl.ds(X * ((z + j) % Z), X)
        write(nw_ref.at[both], nw_hbm.at[both])
    for c in writes:
        c.wait()
    for cond, make in pend:
        when(cond, lambda: make().wait_send())


def place(*refs):
    srcs, dsts, held, sems = refs[:5], refs[5:10], refs[10:15], refs[15]
    into, out = [], []
    for src, dst, buf in zip(srcs, dsts, held):
        step = src.shape[0] // PIECES
        for i in range(PIECES):
            here, j = pl.ds(i * step, step), len(into)
            into.append(pltpu.make_async_copy(src.at[here], buf.at[here], sems.at[0, j]))
            out.append(pltpu.make_async_copy(buf.at[here], dst.at[here], sems.at[1, j]))
    for c in into:
        c.start()
    for c, d in zip(into, out):
        c.wait()
        d.start()
    for d in out:
        d.wait()


def local_kernel(inputs, pre_act, grad_hidden, master, moment_one, moment_two):
    tok, hid = pre_act.shape
    rows = master.shape[0]
    n, half = Z * X, rows // 2
    gb = hid - G_SPLIT
    vmem = pl.BlockSpec(memory_space=pltpu.VMEM)
    dma = pltpu.SemaphoreType.DMA
    anywhere, hbm = pl.BlockSpec(memory_space=pl.ANY), pl.BlockSpec(memory_space=pltpu.HBM)
    out = pl.pallas_call(
        kernel,
        out_shape=(
            jax.ShapeDtypeStruct((tok, rows * X), BF16),
            *[jax.ShapeDtypeStruct((rows, hid), F32)] * 3,
            jax.ShapeDtypeStruct((n, rows, hid), BF16),
        ),
        in_specs=[anywhere, vmem, vmem, vmem, anywhere, anywhere],
        out_specs=[anywhere] * 5,
        scratch_shapes=[
            pltpu.VMEM((tok, rows * X), BF16),
            *[pltpu.VMEM((rows, hid), F32)] * 3,
            pltpu.VMEM((n, rows, hid), BF16),
            pltpu.VMEM((rows, hid), F32),
            pltpu.VMEM((rows, hid), F32),
            pltpu.VMEM((n, tok, rows), BF16),
            pltpu.VMEM((n, rows, hid), BF16),
            pltpu.VMEM((T, X, rows, hid), BF16),
            pltpu.VMEM((T, tok, hid), BF16),
            pltpu.VMEM((hid, tok), BF16),
            pltpu.VMEM((2, n, hid, half), BF16),
            pltpu.VMEM((2, Z, G_SPLIT, half), BF16),
            *[pltpu.VMEM((2, Z - 1, G_SPLIT, half), BF16)] * 4,
            *[pltpu.VMEM((2, Z - 1, X, gb, half), BF16)] * 4,
            pltpu.VMEM((2, X, gb, half), F32),
            pltpu.VMEM((2, 2, gb, half), BF16),
            pltpu.VMEM((2, hid, half), F32),
            dma((tok // 256 + Z + 3,)), dma((2,)), dma((n,)), dma((T - 1,)), dma((T - 1,)),
            dma((Z * X * 2,)), dma((T * X * 2,)),
            dma((2, 17)), dma((2, 17)), dma((2, 17)),
            dma((2, Z)), dma((2, Z)),
            dma((2, 6)), dma((2, 6)), dma((2, 6)), dma((2, 6)),
            dma((2,)), dma((2,)),
        ],
        compiler_params=pltpu.CompilerParams(
            collective_id=0, has_side_effects=True, vmem_limit_bytes=60 * 1024 * 1024
        ),
        cost_estimate=pl.CostEstimate(
            flops=4 * tok * rows * n * hid, bytes_accessed=2 * tok * rows * n * 2, transcendentals=tok * hid
        ),
    )(inputs, pre_act, grad_hidden, master, moment_one, moment_two)
    out = pl.pallas_call(
        place,
        out_shape=tuple(jax.ShapeDtypeStruct(a.shape, a.dtype) for a in out),
        in_specs=[hbm] * 5,
        out_specs=[hbm] * 5,
        scratch_shapes=[*[pltpu.VMEM(a.shape, a.dtype) for a in out], dma((2, 5 * PIECES))],
        compiler_params=pltpu.CompilerParams(vmem_limit_bytes=60 * 1024 * 1024),
        cost_estimate=pl.CostEstimate(flops=0, bytes_accessed=2 * 9 * 2**20, transcendentals=0),
    )(*out)
    return (*out[:4], out[4].reshape(n * rows, hid))


def local_plain(inputs, pre_act, grad_hidden, master, moment_one, moment_two):
    act_grad = (grad_hidden.astype(F32) * gelu_slope(pre_act.astype(F32))).astype(BF16)
    weights = lax.all_gather(master.astype(BF16), "dp", axis=0, tiled=True)
    rows = lax.all_to_all(weights, "tensor", split_axis=0, concat_axis=1, tiled=True)
    acts = lax.all_gather(act_grad, "tensor", axis=1, tiled=True)
    grad_input = jnp.einsum("th,dh->td", acts, rows, preferred_element_type=F32).astype(BF16)
    term = jnp.einsum("tr,th->rh", inputs, act_grad, preferred_element_type=F32)
    codes, scale = encode(term)
    grad = lax.psum_scatter(decode(codes, scale), "dp", scatter_dimension=0, tiled=True)
    new_master, new_one, new_two = adam(grad, master, moment_one, moment_two)
    new_weights = lax.all_gather(new_master.astype(BF16), "dp", axis=0, tiled=True)
    return (grad_input, new_master, new_one, new_two, new_weights)


def solution(mesh):
    sizes = dict(mesh.shape)
    body = local_kernel if sizes == {"dp": Z * X, "tensor": T} else local_plain
    two = P("dp", "tensor")
    return jax.shard_map(
        body,
        mesh=mesh,
        in_specs=(P("dp", None), two, two, two, two, two),
        out_specs=(two, two, two, two, P(None, "tensor")),
        check_vma=False,
    )
```
